32 devices in a mesh: dp: 8 (over z, x), row: 2 (over y), col: 2 (over core).
Axes of the slice: x: 2, y: 2, z: 4, core: 2. Of those that a mesh axis runs over, the one named last changes fastest.
Arguments:
- inputs: bfloat16 [32768, 640], P('dp', ('row', 'col')), may hold values from -6 to 6
- cotangent: bfloat16 [32768, 640], P('dp', ('row', 'col')), may hold values from -6 to 6
- query_weight: bfloat16 [640, 1024], P('row', 'col'), may hold values from -0.25 to 0.25
- keyval_weight: bfloat16 [640, 512], P('row'), may hold values from -0.25 to 0.25
- out_weight: bfloat16 [1024, 640], P('col', 'row'), may hold values from -0.1875 to 0.1875
- gate_weight: bfloat16 [640, 2048], P('row', 'col'), may hold values from -0.25 to 0.25
- up_weight: bfloat16 [640, 2048], P('row', 'col'), may hold values from -0.25 to 0.25
- down_weight: bfloat16 [2048, 640], P('col', 'row'), may hold values from -0.125 to 0.125
- attend_in_gain: float32 [640], P(('row', 'col')), may hold values from -0.4 to 0.4
- attend_out_gain: float32 [640], P(('row', 'col')), may hold values from -0.4 to 0.4
- forward_in_gain: float32 [640], P(('row', 'col')), may hold values from -0.4 to 0.4
- forward_out_gain: float32 [640], P(('row', 'col')), may hold values from -0.4 to 0.4
- query_gain: float32 [256], replicated, may hold values from -0.4 to 0.4
- key_gain: float32 [256], replicated, may hold values from -0.4 to 0.4
Outputs:
- output: bfloat16 [32768, 640], P('dp', ('row', 'col'))
- input_grad: float32 [32768, 640], P('dp', ('row', 'col'))
- query_weight_grad: float32 [640, 1024], P('row', 'col')
- keyval_weight_grad: float32 [640, 512], P('row')
- out_weight_grad: float32 [1024, 640], P('col', 'row')
- gate_weight_grad: float32 [640, 2048], P('row', 'col')
- up_weight_grad: float32 [640, 2048], P('row', 'col')
- down_weight_grad: float32 [2048, 640], P('col', 'row')
- attend_in_gain_grad: float32 [640], P(('row', 'col'))
- attend_out_gain_grad: float32 [640], P(('row', 'col'))
- forward_in_gain_grad: float32 [640], P(('row', 'col'))
- forward_out_gain_grad: float32 [640], P(('row', 'col'))
- query_gain_grad: float32 [256], replicated
- key_gain_grad: float32 [256], replicated
The draws below stay inside these ranges and needn't reach their ends.
All inputs are finite; a program needn't handle non-finite values.
Results may differ from the reference program's by a relative error of at most 0.018.
Values may be sent and summed in bfloat16 or wider, within the bound.
No kernel may reach another device: no remote copies, remote signals or barrier semaphores. Data moves between devices by JAX's collectives and lax.ppermute only.
A program may use at most 192 MiB of HBM per device.

```python
import jax
import jax.numpy as jnp
from jax import lax

D = 640
HEADS = 4
HEAD_DIM = 256
FF = 2048
WINDOW = 512
LEN = 4096
SEQUENCES = 8
TOKENS = 32768


def level_of(rng, extent, pieces, smallest, top_value):
    gain = 1.0
    for dim, shards_of in pieces:
        steps = jax.random.uniform(jax.random.fold_in(jax.random.fold_in(rng, 6), dim), (shards_of,), jnp.float32, smallest / len(pieces), top_value / len(pieces))
        gain = gain * jnp.repeat(jnp.exp(steps), extent[dim] // shards_of).reshape((-1,) + (1,) * (len(extent) - 1 - dim))
    return gain


def bell_draw(key, shape, scale, most, pieces=(), kind=jnp.bfloat16):
    factor_of = level_of(key, shape, pieces, -0.22, 0.18) if pieces else 1.0
    values = jax.random.normal(key, shape, jnp.float32) * scale * factor_of
    return jnp.minimum(jnp.maximum(values, -most), most).astype(kind)


def setup_inputs(seed: int = 0) -> dict:
    seeds = jax.random.split(jax.random.key(seed), 15)
    return {
        "inputs": bell_draw(seeds[0], (TOKENS, D), 1.0, 6.0, ((0, 8), (1, 4))),
        "cotangent": bell_draw(seeds[1], (TOKENS, D), 1.0, 6.0, ((0, 8), (1, 4))),
        "query_weight": bell_draw(seeds[2], (D, HEADS * HEAD_DIM), D ** -0.5, 0.25, ((0, 2), (1, 2))),
        "keyval_weight": bell_draw(seeds[3], (D, 2 * HEAD_DIM), D ** -0.5, 0.25, ((0, 2),)),
        "out_weight": bell_draw(seeds[4], (HEADS * HEAD_DIM, D), (HEADS * HEAD_DIM) ** -0.5, 0.1875, ((0, 2), (1, 2))),
        "gate_weight": bell_draw(seeds[5], (D, FF), D ** -0.5, 0.25, ((0, 2), (1, 2))),
        "up_weight": bell_draw(seeds[6], (D, FF), D ** -0.5, 0.25, ((0, 2), (1, 2))),
        "down_weight": bell_draw(seeds[7], (FF, D), FF ** -0.5, 0.125, ((0, 2), (1, 2))),
        "attend_in_gain": jnp.clip(jax.random.uniform(seeds[8], (D,), jnp.float32, -0.4, 0.4) * level_of(seeds[8], (D,), ((0, 4),), -0.4, 0.0), -0.4, 0.4),
        "attend_out_gain": jnp.clip(jax.random.uniform(seeds[9], (D,), jnp.float32, -0.4, 0.4) * level_of(seeds[9], (D,), ((0, 4),), -0.4, 0.0), -0.4, 0.4),
        "forward_in_gain": jnp.clip(jax.random.uniform(seeds[10], (D,), jnp.float32, -0.4, 0.4) * level_of(seeds[10], (D,), ((0, 4),), -0.4, 0.0), -0.4, 0.4),
        "forward_out_gain": jnp.clip(jax.random.uniform(seeds[11], (D,), jnp.float32, -0.4, 0.4) * level_of(seeds[11], (D,), ((0, 4),), -0.4, 0.0), -0.4, 0.4),
        "query_gain": jnp.clip(jax.random.uniform(seeds[12], (HEAD_DIM,), jnp.float32, -0.4, 0.4), -0.4, 0.4),
        "key_gain": jnp.clip(jax.random.uniform(seeds[13], (HEAD_DIM,), jnp.float32, -0.4, 0.4), -0.4, 0.4),
    }


EPSILON = 1e-06
ROPE_BASE = 10000.0
MASKED = -1e+30
HIGHEST = lax.Precision.HIGHEST

@jax.custom_vjp
def low(v):
    return lax.optimization_barrier(v.astype(jnp.bfloat16)).astype(jnp.float32)

@jax.custom_vjp
def low_back(v):
    return v

def low_keep(v):
    return (low(v), None)

def low_pass(kept, grad):
    return (grad,)

def back_keep(v):
    return (v, None)

def back_low(kept, grad):
    return (low(grad),)
low.defvjp(low_keep, low_pass)
low_back.defvjp(back_keep, back_low)

def rms_scale(values, offset):
    mean_sq = lax.optimization_barrier(jnp.mean(values * values, axis=-1, keepdims=True))
    return values * lax.rsqrt(mean_sq + EPSILON) * (1.0 + offset)

def rotate(values, cosine, sine):
    half_dim = values.shape[-1] // 2
    first_half = values[..., :half_dim]
    second_half = values[..., half_dim:]
    return jnp.concatenate([first_half * cosine - second_half * sine, second_half * cosine + first_half * sine], axis=-1)

def rope_tables():
    half_dim = HEAD_DIM // 2
    frequency = ROPE_BASE ** (-(jnp.arange(half_dim, dtype=jnp.float32) * 2.0 / HEAD_DIM))
    angles = jnp.arange(LEN, dtype=jnp.float32)[:, None] * frequency[None, :]
    return (jnp.cos(angles), jnp.sin(angles))

def attend_block(query_block, key_window, value_window, first_row):
    block_rows = query_block.shape[1]
    key_span = key_window.shape[0]
    scores = low_back(jnp.einsum('hqd,kd->hqk', query_block, key_window, precision=HIGHEST))
    query_pos = first_row + jnp.arange(block_rows, dtype=jnp.int32)[:, None]
    key_pos = first_row - WINDOW + jnp.arange(key_span, dtype=jnp.int32)[None, :]
    keep_mask = (query_pos - key_pos < WINDOW) & (query_pos >= key_pos) & (key_pos >= 0)
    masked = jnp.where(keep_mask[None], scores, MASKED)
    row_max = lax.optimization_barrier(jnp.max(masked, axis=-1, keepdims=True))
    weights = jnp.exp(masked - row_max)
    softmax_out = low(weights / lax.optimization_barrier(jnp.sum(weights, axis=-1, keepdims=True)))
    return jnp.einsum('hqk,kd->hqd', softmax_out, value_window, precision=HIGHEST)

def layer(residual, query_weight, keyval_weight, out_weight, gate_weight, up_weight, down_weight, attend_in_gain, attend_out_gain, forward_in_gain, forward_out_gain, query_gain, key_gain):
    cosine, sine = rope_tables()
    attend_in = low(rms_scale(residual, attend_in_gain))
    query_raw = low_back(jnp.dot(attend_in, query_weight, precision=HIGHEST)).reshape(LEN, HEADS, HEAD_DIM)
    keyval_raw = jnp.dot(attend_in, keyval_weight, precision=HIGHEST)
    key_raw = low_back(keyval_raw[:, :HEAD_DIM])
    value_rows = low(low_back(keyval_raw[:, HEAD_DIM:]))
    query_rows = low(rotate(rms_scale(query_raw, query_gain), cosine[:, None, :], sine[:, None, :]) * HEAD_DIM ** (-0.5))
    key_rows = low(rotate(rms_scale(key_raw, key_gain), cosine, sine))
    block_rows = min(512, LEN // 2)
    block_count = LEN // block_rows
    key_pad = jnp.pad(key_rows, ((WINDOW, 0), (0, 0)))
    value_pad = jnp.pad(value_rows, ((WINDOW, 0), (0, 0)))
    query_blocks = query_rows.transpose(1, 0, 2).reshape(HEADS, block_count, block_rows, HEAD_DIM).transpose(1, 0, 2, 3)
    block_starts = jnp.arange(block_count, dtype=jnp.int32) * block_rows
    block_function = jax.checkpoint(attend_block)

    def one_block(paired):
        query_block, first_row = paired
        key_window = lax.dynamic_slice_in_dim(key_pad, first_row, block_rows + WINDOW, 0)
        value_window = lax.dynamic_slice_in_dim(value_pad, first_row, block_rows + WINDOW, 0)
        return block_function(query_block, key_window, value_window, first_row)
    attended = lax.map(one_block, (query_blocks, block_starts))
    mixed_heads = low(low_back(attended.transpose(0, 2, 1, 3).reshape(LEN, HEADS * HEAD_DIM)))
    branch_attn = low_back(jnp.dot(mixed_heads, out_weight, precision=HIGHEST))
    hidden_state = residual + rms_scale(branch_attn, attend_out_gain)
    forward_in = low(rms_scale(hidden_state, forward_in_gain))
    gate_value = low_back(jnp.dot(forward_in, gate_weight, precision=HIGHEST))
    up_value = low_back(jnp.dot(forward_in, up_weight, precision=HIGHEST))
    product = low(jax.nn.gelu(gate_value, approximate=True) * up_value)
    branch_ffn = low_back(jnp.dot(product, down_weight, precision=HIGHEST))
    return hidden_state + rms_scale(branch_ffn, forward_out_gain)

def reference(inputs, cotangent, query_weight, keyval_weight, out_weight, gate_weight, up_weight, down_weight, attend_in_gain, attend_out_gain, forward_in_gain, forward_out_gain, query_gain, key_gain):
    params = tuple((weight_array.astype(jnp.float32) for weight_array in (query_weight, keyval_weight, out_weight, gate_weight, up_weight, down_weight, attend_in_gain, attend_out_gain, forward_in_gain, forward_out_gain, query_gain, key_gain)))
    residual_seq = inputs.astype(jnp.float32).reshape(SEQUENCES, LEN, D)
    upstream_seq = cotangent.astype(jnp.float32).reshape(SEQUENCES, LEN, D)

    def one_sequence(totals, paired):
        residual, upstream = paired
        result, pullback = jax.vjp(layer, residual, params[0], params[1], params[2], params[3], params[4], params[5], params[6], params[7], params[8], params[9], params[10], params[11])
        gradients = pullback(upstream)
        summed = tuple((running + fresh for running, fresh in zip(totals, gradients[1:])))
        return (summed, (result.astype(jnp.bfloat16), gradients[0]))
    start_totals = tuple((jnp.zeros_like(weight_array) for weight_array in params))
    totals, (outputs, input_grads) = lax.scan(one_sequence, start_totals, (residual_seq, upstream_seq))
    return (outputs.reshape(TOKENS, D), input_grads.reshape(TOKENS, D), totals[0], totals[1], totals[2], totals[3], totals[4], totals[5], totals[6], totals[7], totals[8], totals[9], totals[10], totals[11])
```

```python
from functools import partial

import jax
import jax.numpy as jnp
from jax import lax
from jax.experimental import pallas as pl
from jax.experimental.pallas import tpu as pltpu
from jax.sharding import PartitionSpec as P

D = 640
HEADS = 4
HEAD_DIM = 256
WINDOW = 512
LEN = 4096
PARTS = 4
BLOCK = 256
SPAN = BLOCK + WINDOW

EPSILON = 1e-06
ROPE_BASE = 10000.0

F32 = jnp.float32
BF16 = jnp.bfloat16


def swap(values, axis):
    return lax.ppermute(values, axis, [(0, 1), (1, 0)])


def swap_dp(values, bit):
    size = lax.axis_size("dp")
    return lax.ppermute(values, "dp", [(i, i ^ bit) for i in range(size)])


def ordered(flag, own, other, axis):
    first = jnp.where(flag == 0, own, other)
    second = jnp.where(flag == 0, other, own)
    return jnp.concatenate([first, second], axis=axis)


def exchange(blocks, part):
    got = [lax.dynamic_index_in_dim(blocks, part, 0, keepdims=False)]
    for k in (1, 2, 3):
        sent = lax.dynamic_index_in_dim(blocks, part ^ k, 0, keepdims=False)
        got.append(lax.ppermute(sent, ("row", "col"), [(i, i ^ k) for i in range(PARTS)]))
    return got


def to_tokens(values, part, col):
    tokens = values.shape[0] // PARTS
    got = exchange(values.reshape(PARTS, tokens, values.shape[1]), part)
    return jnp.concatenate(
        [ordered(col, got[0], got[1], 1), ordered(col, got[2], got[3], 1)], axis=1
    )


def to_features(values, part, col):
    tokens = values.shape[0]
    width = values.shape[1] // PARTS
    quarters = [values[:, i * width : (i + 1) * width] for i in range(PARTS)]
    own = [jnp.where(col == 0, quarters[0], quarters[1]), jnp.where(col == 0, quarters[1], quarters[0])]
    far = [jnp.where(col == 0, quarters[2], quarters[3]), jnp.where(col == 0, quarters[3], quarters[2])]
    sent = own + far
    got = [sent[0]]
    for k in (1, 2, 3):
        got.append(lax.ppermute(sent[k], ("row", "col"), [(i, i ^ k) for i in range(PARTS)]))
    out = jnp.zeros((PARTS, tokens, width), values.dtype)
    for k in range(PARTS):
        out = lax.dynamic_update_index_in_dim(out, got[k], part ^ k, 0)
    return out.reshape(PARTS * tokens, width)


def gather_gains(gains, col):
    half = ordered(col, gains, swap(gains, "col"), 1)
    return jnp.concatenate([half, swap(half, "row")], axis=1)


def gather_weight(shard):
    tall = jnp.concatenate([shard, swap(shard, "row")], axis=0)
    return jnp.concatenate([tall, swap(tall, "col")], axis=1)


def reduce_gradient(grad):
    rows, cols = grad.shape
    low = grad.astype(BF16)
    half = grad[:, : cols // 2] + swap(low[:, cols // 2 :], "col").astype(F32)
    low = half[rows // 2 :].astype(BF16)
    total = half[: rows // 2] + swap(low, "row").astype(F32)
    return all_reduce_dp(total)


def all_reduce_dp(total):
    size = lax.axis_size("dp")
    me = lax.axis_index("dp")
    bit = 1
    steps = []
    while bit < size:
        axis = 1 if total.shape[1] % 256 == 0 else 0
        length = total.shape[axis] // 2
        mine = (me // bit) % 2
        keep = lax.dynamic_slice_in_dim(total, mine * length, length, axis)
        send = lax.dynamic_slice_in_dim(total, (1 - mine) * length, length, axis)
        total = keep + swap_dp(send.astype(BF16), bit).astype(F32)
        steps.append((bit, axis, mine))
        bit *= 2
    result = total.astype(BF16)
    for bit, axis, mine in reversed(steps):
        result = ordered(mine, result, swap_dp(result, bit), axis)
    return result.astype(F32)


def scale_of(values):
    return lax.rsqrt(jnp.mean(values * values, axis=-1, keepdims=True) + EPSILON)


def norm_backward(values, scale, offset, gradient):
    unit = values * scale
    scaled = gradient * (1.0 + offset)
    inner = jnp.mean(scaled * unit, axis=-1, keepdims=True)
    return scale * (scaled - unit * inner), jnp.sum(gradient * unit, axis=0)


def rms_scale(values, offset):
    return values * scale_of(values) * (1.0 + offset)


def rotate(values, cosine, sine):
    half_dim = values.shape[-1] // 2
    first_half = values[..., :half_dim]
    second_half = values[..., half_dim:]
    return jnp.concatenate(
        [first_half * cosine - second_half * sine, second_half * cosine + first_half * sine],
        axis=-1,
    )


def rope_tables(first, count):
    half_dim = HEAD_DIM // 2
    frequency = ROPE_BASE ** (-(jnp.arange(half_dim, dtype=F32) * 2.0 / HEAD_DIM))
    angles = (first + jnp.arange(count, dtype=jnp.int32)).astype(F32)[:, None] * frequency[None, :]
    return (jnp.cos(angles), jnp.sin(angles))


def nn(a, b):
    return jnp.dot(a, b, preferred_element_type=F32)


def nt(a, b):
    return lax.dot_general(a, b, (((1,), (1,)), ((), ())), preferred_element_type=F32)


def tn(a, b):
    return lax.dot_general(a, b, (((0,), (0,)), ((), ())), preferred_element_type=F32)


def seen_mask(first_key):
    key = lax.broadcasted_iota(jnp.int32, (SPAN, BLOCK), 0)
    query = lax.broadcasted_iota(jnp.int32, (SPAN, BLOCK), 1)
    return (key > query) & (key <= query + WINDOW) & (key >= first_key)


def attend_kernel(first_ref, query_ref, key_ref, value_ref, out_ref):
    block = pl.program_id(0)
    start = pl.multiple_of(block * BLOCK, BLOCK)
    keys = key_ref[pl.ds(start, SPAN), :]
    values = value_ref[pl.ds(start, SPAN), :]
    mask = seen_mask(first_ref[0] - start)
    for head in range(HEADS):
        columns = slice(head * HEAD_DIM, (head + 1) * HEAD_DIM)
        scores = nt(keys, query_ref[:, columns])
        weights = jnp.where(mask, jnp.exp(scores), 0.0)
        total = jnp.sum(weights, axis=0, keepdims=True)
        probs = (weights * (1.0 / total)).astype(BF16)
        out_ref[:, columns] = tn(probs, values).astype(BF16)


def attend_back_kernel(first_ref, query_ref, key_ref, value_ref, grad_ref, query_out, key_out, value_out):
    block = pl.program_id(0)
    start = pl.multiple_of(block * BLOCK, BLOCK)
    window = pl.ds(start, SPAN)
    keys = key_ref[window, :]
    values = value_ref[window, :]
    mask = seen_mask(first_ref[0] - start)

    @pl.when(block == 0)
    def _():
        key_out[...] = jnp.zeros_like(key_out)
        value_out[...] = jnp.zeros_like(value_out)

    key_sum = key_out[window, :]
    value_sum = value_out[window, :]
    for head in range(HEADS):
        columns = slice(head * HEAD_DIM, (head + 1) * HEAD_DIM)
        queries = query_ref[:, columns]
        grads = grad_ref[:, columns]
        weights = jnp.where(mask, jnp.exp(nt(keys, queries)), 0.0)
        probs = weights * (1.0 / jnp.sum(weights, axis=0, keepdims=True))
        prob_grad = nt(values, grads)
        inner = jnp.sum(prob_grad * probs, axis=0, keepdims=True)
        score_grad = (probs * (prob_grad - inner)).astype(BF16)
        query_out[:, columns] = tn(score_grad, keys)
        key_sum += nn(score_grad, queries)
        value_sum += nn(probs.astype(BF16), grads)
    key_out[window, :] = key_sum
    value_out[window, :] = value_sum


def attend(first, query_rows, keys, values):
    tokens, width = query_rows.shape
    span = keys.shape[0]
    return pl.pallas_call(
        attend_kernel,
        grid=(tokens // BLOCK,),
        in_specs=[
            pl.BlockSpec(memory_space=pltpu.SMEM),
            pl.BlockSpec((BLOCK, width), lambda i: (i, 0)),
            pl.BlockSpec((span, HEAD_DIM), lambda i: (0, 0)),
            pl.BlockSpec((span, HEAD_DIM), lambda i: (0, 0)),
        ],
        out_specs=pl.BlockSpec((BLOCK, width), lambda i: (i, 0)),
        out_shape=jax.ShapeDtypeStruct((tokens, width), BF16),
        compiler_params=pltpu.CompilerParams(vmem_limit_bytes=32 << 20),
        cost_estimate=pl.CostEstimate(
            flops=4 * tokens * width * SPAN, bytes_accessed=4 * tokens * width + 4 * span * HEAD_DIM, transcendentals=tokens * HEADS * SPAN
        ),
        name="attend",
    )(first, query_rows, keys, values)


def attend_back(first, query_rows, keys, values, heads_grad):
    tokens, width = query_rows.shape
    span = keys.shape[0]
    return pl.pallas_call(
        attend_back_kernel,
        grid=(tokens // BLOCK,),
        in_specs=[
            pl.BlockSpec(memory_space=pltpu.SMEM),
            pl.BlockSpec((BLOCK, width), lambda i: (i, 0)),
            pl.BlockSpec((span, HEAD_DIM), lambda i: (0, 0)),
            pl.BlockSpec((span, HEAD_DIM), lambda i: (0, 0)),
            pl.BlockSpec((BLOCK, width), lambda i: (i, 0)),
        ],
        out_specs=[
            pl.BlockSpec((BLOCK, width), lambda i: (i, 0)),
            pl.BlockSpec((span, HEAD_DIM), lambda i: (0, 0)),
            pl.BlockSpec((span, HEAD_DIM), lambda i: (0, 0)),
        ],
        out_shape=[
            jax.ShapeDtypeStruct((tokens, width), F32),
            jax.ShapeDtypeStruct((span, HEAD_DIM), F32),
            jax.ShapeDtypeStruct((span, HEAD_DIM), F32),
        ],
        compiler_params=pltpu.CompilerParams(vmem_limit_bytes=32 << 20),
        cost_estimate=pl.CostEstimate(
            flops=10 * tokens * width * SPAN, bytes_accessed=8 * tokens * width + 12 * span * HEAD_DIM, transcendentals=tokens * HEADS * SPAN
        ),
        name="attend_back",
    )(first, query_rows, keys, values, heads_grad)


def per_device(
    inputs,
    cotangent,
    query_weight,
    keyval_weight,
    out_weight,
    gate_weight,
    up_weight,
    down_weight,
    attend_in_gain,
    attend_out_gain,
    forward_in_gain,
    forward_out_gain,
    query_gain,
    key_gain,
):
    assert inputs.shape[0] == LEN
    row = lax.axis_index("row")
    col = lax.axis_index("col")
    part = row * 2 + col
    tokens = LEN // PARTS
    ahead = [(i, i + 1) for i in range(PARTS - 1)]
    behind = [(i + 1, i) for i in range(PARTS - 1)]

    residual_low = to_tokens(inputs, part, col)
    keyval_full = jnp.concatenate([keyval_weight, swap(keyval_weight, "row")], axis=0)
    query_full = gather_weight(query_weight)
    gains = jnp.stack([attend_in_gain, attend_out_gain, forward_in_gain, forward_out_gain])
    gains = gather_gains(gains, col)
    attend_in_gain, attend_out_gain, forward_in_gain, forward_out_gain = (gains[i] for i in range(4))
    out_full = gather_weight(out_weight.T)
    gate_full = gather_weight(gate_weight)
    up_full = gather_weight(up_weight)
    down_full = gather_weight(down_weight.T)
    upstream = to_tokens(cotangent, part, col).astype(F32)

    cosine, sine = rope_tables(part * tokens, tokens)
    first = jnp.where(part == 0, WINDOW, 0).astype(jnp.int32).reshape(1)

    residual = residual_low.astype(F32)
    scale_in = scale_of(residual)
    attend_in = (residual * scale_in * (1.0 + attend_in_gain)).astype(BF16)
    keyval_raw = nn(attend_in, keyval_full)
    key_raw = keyval_raw[:, :HEAD_DIM]
    value_rows = keyval_raw[:, HEAD_DIM:].astype(BF16)

    def query_prep(raw, gain):
        return rotate(rms_scale(raw, gain), cosine[:, None, :], sine[:, None, :]) * HEAD_DIM ** (-0.5)

    def key_prep(raw, gain):
        return rotate(rms_scale(raw, gain), cosine, sine)

    key_ready, key_pullback = jax.vjp(key_prep, key_raw, key_gain)
    key_rows = key_ready.astype(BF16)
    halo = lax.ppermute(
        jnp.concatenate([key_rows[tokens - WINDOW :], value_rows[tokens - WINDOW :]], axis=1),
        ("row", "col"),
        ahead,
    )
    query_raw = nn(attend_in, query_full).reshape(tokens, HEADS, HEAD_DIM)
    query_ready, query_pullback = jax.vjp(query_prep, query_raw, query_gain)
    query_rows = query_ready.astype(BF16).reshape(tokens, HEADS * HEAD_DIM)
    keys = jnp.concatenate([halo[:, :HEAD_DIM], key_rows], axis=0)
    values = jnp.concatenate([halo[:, HEAD_DIM:], value_rows], axis=0)
    mixed_heads = attend(first, query_rows, keys, values)

    branch_attn = nt(mixed_heads, out_full)
    scale_attn = scale_of(branch_attn)
    hidden_state = residual + branch_attn * scale_attn * (1.0 + attend_out_gain)
    scale_mid = scale_of(hidden_state)
    forward_in = (hidden_state * scale_mid * (1.0 + forward_in_gain)).astype(BF16)
    gate_value = nn(forward_in, gate_full)
    up_value = nn(forward_in, up_full)
    activated, gelu_pullback = jax.vjp(partial(jax.nn.gelu, approximate=True), gate_value)
    product = (activated * up_value).astype(BF16)
    branch_ffn = nt(product, down_full)
    scale_out = scale_of(branch_ffn)
    output = (hidden_state + branch_ffn * scale_out * (1.0 + forward_out_gain)).astype(BF16)
    output = to_features(output, part, col)

    ffn_grad, forward_out_grad = norm_backward(branch_ffn, scale_out, forward_out_gain, upstream)
    ffn_grad = ffn_grad.astype(BF16)
    down_grad = reduce_gradient(tn(ffn_grad, product))
    product_grad = nn(ffn_grad, down_full)
    gate_grad = gelu_pullback(product_grad * up_value)[0].astype(BF16)
    up_grad = (product_grad * activated).astype(BF16)
    gate_weight_grad = reduce_gradient(tn(forward_in, gate_grad))
    up_weight_grad = reduce_gradient(tn(forward_in, up_grad))
    mid_grad = nt(gate_grad, gate_full) + nt(up_grad, up_full)
    state_part, forward_in_grad = norm_backward(hidden_state, scale_mid, forward_in_gain, mid_grad)
    state_grad = upstream + state_part
    attn_grad, attend_out_grad = norm_backward(branch_attn, scale_attn, attend_out_gain, state_grad)
    attn_grad = attn_grad.astype(BF16)
    out_grad = reduce_gradient(tn(attn_grad, mixed_heads))
    heads_grad = nn(attn_grad, out_full).astype(BF16)
    query_back, key_back, value_back = attend_back(first, query_rows, keys, values, heads_grad)

    back = lax.ppermute(
        jnp.concatenate([key_back[:WINDOW], value_back[:WINDOW]], axis=1).astype(BF16),
        ("row", "col"),
        behind,
    ).astype(F32)
    query_raw_grad, query_gain_grad = query_pullback(query_back.reshape(tokens, HEADS, HEAD_DIM))
    query_raw_grad = query_raw_grad.reshape(tokens, HEADS * HEAD_DIM).astype(BF16)
    query_grad = tn(attend_in, query_raw_grad)
    in_query = nt(query_raw_grad, query_full)

    rest = tokens - WINDOW
    key_own = jnp.concatenate([key_back[WINDOW : WINDOW + rest], key_back[tokens:] + back[:, :HEAD_DIM]], axis=0)
    value_own = jnp.concatenate([value_back[WINDOW : WINDOW + rest], value_back[tokens:] + back[:, HEAD_DIM:]], axis=0)
    key_raw_grad, key_gain_grad = key_pullback(key_own)
    keyval_raw_grad = jnp.concatenate([key_raw_grad, value_own], axis=1).astype(BF16)
    keyval_grad = tn(attend_in, keyval_raw_grad)
    in_grad = in_query + nt(keyval_raw_grad, keyval_full)
    residual_part, attend_in_grad = norm_backward(residual, scale_in, attend_in_gain, in_grad)
    input_grad = to_features((state_grad + residual_part).astype(BF16), part, col).astype(F32)

    query_grad = reduce_gradient(query_grad)
    keyval_mine = lax.dynamic_slice_in_dim(keyval_grad, col * HEAD_DIM, HEAD_DIM, 1)
    keyval_sent = lax.dynamic_slice_in_dim(keyval_grad, (1 - col) * HEAD_DIM, HEAD_DIM, 1)
    keyval_total = reduce_gradient(jnp.concatenate([keyval_mine, keyval_sent], axis=1))
    keyval_total = ordered(col, keyval_total, swap(keyval_total, "col"), 1)

    gain_rows = jnp.concatenate(
        [attend_in_grad, attend_out_grad, forward_in_grad, forward_out_grad, query_gain_grad, key_gain_grad]
    )
    rows4 = gain_rows[: 4 * D].reshape(4, D)
    half = rows4.reshape(4, 2, 2, D // 4)
    mine = lax.dynamic_index_in_dim(half[:, 0], col, 1, keepdims=False)
    others = [
        lax.dynamic_index_in_dim(half[:, 0], 1 - col, 1, keepdims=False),
        lax.dynamic_index_in_dim(half[:, 1], col, 1, keepdims=False),
        lax.dynamic_index_in_dim(half[:, 1], 1 - col, 1, keepdims=False),
    ]
    gain_total = mine
    for k in (1, 2, 3):
        gain_total = gain_total + lax.ppermute(others[k - 1], ("row", "col"), [(i, i ^ k) for i in range(PARTS)])
    small = gain_rows[4 * D :]
    small = small + swap(small, "col")
    small = small + swap(small, "row")
    packed = jnp.concatenate([gain_total.reshape(-1), small])
    packed = lax.psum(packed, "dp")
    gain_total = packed[:D].reshape(4, D // 4)
    query_gain_grad = packed[D : D + HEAD_DIM]
    key_gain_grad = packed[D + HEAD_DIM :]
    return (
        output,
        input_grad,
        query_grad,
        keyval_total,
        out_grad.T,
        gate_weight_grad,
        up_weight_grad,
        down_grad.T,
        gain_total[0],
        gain_total[1],
        gain_total[2],
        gain_total[3],
        query_gain_grad,
        key_gain_grad,
    )


def solution(mesh):
    wide = P("dp", ("row", "col"))
    gain = P(("row", "col"))
    weights = (P("row", "col"), P("row", None), P("col", "row"), P("row", "col"), P("row", "col"), P("col", "row"))
    gains = (gain, gain, gain, gain, P(), P())
    return jax.shard_map(
        per_device,
        mesh=mesh,
        in_specs=(wide, wide) + weights + gains,
        out_specs=(wide, wide) + weights + gains,
        check_vma=False,
    )
```

```python
import jax
import jax.numpy as jnp
from jax import lax
from jax.experimental import pallas as pl
from jax.experimental.pallas import tpu as pltpu
from jax.sharding import PartitionSpec as P

D = 640
HEADS = 4
HEAD_DIM = 256
WINDOW = 512
LEN = 4096
PARTS = 4
BLOCK = 256
SPAN = BLOCK + WINDOW

EPSILON = 1e-06
ROPE_BASE = 10000.0

F32 = jnp.float32
BF16 = jnp.bfloat16


def pin(*values):
    return lax.optimization_barrier(values)


def swap(values, axis):
    return lax.ppermute(values, axis, [(0, 1), (1, 0)])


def swap_dp(values, bit):
    size = lax.axis_size("dp")
    return lax.ppermute(values, "dp", [(i, i ^ bit) for i in range(size)])


def swap_part(values, k):
    return lax.ppermute(values, ("row", "col"), [(i, i ^ k) for i in range(PARTS)])


def ordered(flag, own, other, axis):
    first = jnp.where(flag == 0, own, other)
    second = jnp.where(flag == 0, other, own)
    return jnp.concatenate([first, second], axis=axis)


def half_of(values, index, axis):
    length = values.shape[axis] // 2
    return lax.dynamic_slice_in_dim(values, index * length, length, axis)


def to_tokens(values, part, col):
    tokens = values.shape[1] // PARTS

    def block(k):
        return lax.dynamic_slice_in_dim(values, (part ^ k) * tokens, tokens, 1)

    got = [block(0)] + [swap_part(block(k), k) for k in (1, 2, 3)]
    return jnp.concatenate(
        [ordered(col, got[0], got[1], 0), ordered(col, got[2], got[3], 0)], axis=0
    )


def send_features(values, col):
    width = values.shape[0] // PARTS
    quarters = [values[i * width : (i + 1) * width] for i in range(PARTS)]
    sent = []
    for pair in (quarters[:2], quarters[2:]):
        sent.append(jnp.where(col == 0, pair[0], pair[1]))
        sent.append(jnp.where(col == 0, pair[1], pair[0]))
    return [sent[0]] + [swap_part(sent[k], k) for k in (1, 2, 3)]


def join_features(got, part):
    out = []
    for block in range(PARTS):
        piece = got[0]
        for k in (1, 2, 3):
            piece = jnp.where((part ^ k) == block, got[k], piece)
        out.append(piece)
    return jnp.concatenate(out, axis=1)


def gather_gains(gains, col):
    half = ordered(col, gains, swap(gains, "col"), 1)
    return jnp.concatenate([half, swap(half, "row")], axis=1)


def grid4(own, own_col, other, other_col):
    return jnp.concatenate(
        [jnp.concatenate([own, own_col], axis=1), jnp.concatenate([other, other_col], axis=1)], axis=0
    )


def dp_half(total):
    mine = lax.axis_index("dp") % 2
    axis = total.ndim - 1
    return half_of(total, mine, axis), swap_dp(half_of(total, 1 - mine, axis).astype(BF16), 1)


def row_half(total):
    rows = total.shape[0] // 2
    return total[:rows], swap(total[rows:].astype(BF16), "row")


def dp_groups(step):
    return [list(range(i, lax.axis_size("dp"), step)) for i in range(step)]


def spread(total, step):
    groups = dp_groups(step)
    count = len(groups[0])
    rows, cols = total.shape
    shares = total.astype(BF16).reshape(count, rows // count, cols)
    return lax.all_to_all(shares, "dp", 0, 0, tiled=True, axis_index_groups=groups)


def collect(shares, step):
    count, rows, cols = shares.shape
    share = jnp.sum(shares.astype(F32), axis=0, keepdims=True).astype(BF16)
    whole = lax.all_to_all(
        jnp.broadcast_to(share, shares.shape), "dp", 0, 0, tiled=True, axis_index_groups=dp_groups(step)
    )
    return whole.reshape(count * rows, cols)


def dp_whole(half):
    return ordered(lax.axis_index("dp") % 2, half, swap_dp(half, 1), 1)


def scale_of(values):
    return lax.rsqrt(jnp.mean(values * values, axis=-2, keepdims=True) + EPSILON)


def norm_backward(values, scale, offset, gradient):
    unit = values * scale
    scaled = gradient * (1.0 + offset)
    inner = jnp.mean(scaled * unit, axis=0, keepdims=True)
    return scale * (scaled - unit * inner), jnp.sum(gradient * unit, axis=1, keepdims=True)


def rms_scale(values, offset):
    return values * scale_of(values) * (1.0 + offset)


def rotate(values, cosine, sine):
    half_dim = values.shape[-2] // 2
    first_half = values[..., :half_dim, :]
    second_half = values[..., half_dim:, :]
    return jnp.concatenate(
        [first_half * cosine - second_half * sine, second_half * cosine + first_half * sine],
        axis=-2,
    )


def rope_tables(first, count):
    half_dim = HEAD_DIM // 2
    frequency = ROPE_BASE ** (-(jnp.arange(half_dim, dtype=F32) * 2.0 / HEAD_DIM))
    angles = (first + jnp.arange(count, dtype=jnp.int32)).astype(F32)[None, :] * frequency[:, None]
    return (jnp.cos(angles), jnp.sin(angles))


def nn(a, b):
    return jnp.dot(a, b, preferred_element_type=F32)


def nt(a, b):
    return lax.dot_general(a, b, (((1,), (1,)), ((), ())), preferred_element_type=F32)


def tn(a, b):
    return lax.dot_general(a, b, (((0,), (0,)), ((), ())), preferred_element_type=F32)


def seen_mask(first_key):
    key = lax.broadcasted_iota(jnp.int32, (SPAN, BLOCK), 0)
    query = lax.broadcasted_iota(jnp.int32, (SPAN, BLOCK), 1)
    return (key > query) & (key <= query + WINDOW) & (key >= first_key)


def attend_kernel(first_ref, query_ref, key_ref, value_ref, out_ref):
    start = pl.multiple_of(pl.program_id(0) * BLOCK, BLOCK)
    keys = key_ref[:, pl.ds(start, SPAN)].T
    values = value_ref[:, pl.ds(start, SPAN)]
    mask = seen_mask(first_ref[0] - start)
    for head in range(HEADS):
        features = slice(head * HEAD_DIM, (head + 1) * HEAD_DIM)
        weights = jnp.where(mask, jnp.exp(nn(keys, query_ref[features, :])), 0.0)
        total = jnp.sum(weights, axis=0, keepdims=True)
        probs = (weights * (1.0 / total)).astype(BF16)
        out_ref[features, :] = nn(values, probs).astype(BF16)


def attend_back_kernel(first_ref, query_ref, key_ref, value_ref, grad_ref, query_out, key_out, value_out):
    block = pl.program_id(0)
    start = pl.multiple_of(block * BLOCK, BLOCK)
    window = pl.ds(start, SPAN)
    keys_wide = key_ref[:, window]
    keys = keys_wide.T
    values = value_ref[:, window].T
    mask = seen_mask(first_ref[0] - start)

    @pl.when(block == 0)
    def _():
        key_out[...] = jnp.zeros_like(key_out)
        value_out[...] = jnp.zeros_like(value_out)

    key_sum = key_out[:, window]
    value_sum = value_out[:, window]
    for head in range(HEADS):
        features = slice(head * HEAD_DIM, (head + 1) * HEAD_DIM)
        queries = query_ref[features, :]
        grads = grad_ref[features, :]
        weights = jnp.where(mask, jnp.exp(nn(keys, queries)), 0.0)
        probs = weights * (1.0 / jnp.sum(weights, axis=0, keepdims=True))
        prob_grad = nn(values, grads)
        inner = jnp.sum(prob_grad * probs, axis=0, keepdims=True)
        score_grad = (probs * (prob_grad - inner)).astype(BF16)
        query_out[features, :] = nn(keys_wide, score_grad)
        key_sum += nt(queries, score_grad)
        value_sum += nt(grads, probs.astype(BF16))
    key_out[:, window] = key_sum
    value_out[:, window] = value_sum


def attend_call(kernel, name, out_specs, out_shape, products, arrays):
    width, tokens = arrays[1].shape
    span = arrays[2].shape[1]
    block = pl.BlockSpec((width, BLOCK), lambda i: (0, i))
    whole = pl.BlockSpec((HEAD_DIM, span), lambda i: (0, 0))
    return pl.pallas_call(
        kernel,
        grid=(tokens // BLOCK,),
        in_specs=[pl.BlockSpec(memory_space=pltpu.SMEM), block, whole, whole] + [block] * (len(arrays) - 4),
        out_specs=[{"block": block, "whole": whole}[spec] for spec in out_specs],
        out_shape=out_shape,
        compiler_params=pltpu.CompilerParams(vmem_limit_bytes=32 << 20),
        cost_estimate=pl.CostEstimate(
            flops=2 * products * tokens * width * SPAN,
            bytes_accessed=4 * tokens * width,
            transcendentals=tokens * HEADS * SPAN,
        ),
        name=name,
    )(*arrays)


def attend(first, queries, keys, values):
    shape = [jax.ShapeDtypeStruct(queries.shape, BF16)]
    return attend_call(attend_kernel, "attend", ["block"], shape, 2, (first, queries, keys, values))[0]


def attend_back(first, queries, keys, values, heads_grad):
    shapes = [jax.ShapeDtypeStruct(a.shape, F32) for a in (queries, keys, values)]
    return attend_call(
        attend_back_kernel,
        "attend_back",
        ["block", "whole", "whole"],
        shapes,
        5,
        (first, queries, keys, values, heads_grad),
    )


HIDDEN = 256
GELU_SCALE = 0.7978845608028654
GELU_CUBE = 0.044715


def ffn_kernel(x_ref, gate_own, gate_far, up_own, up_far, down_own, down_far, gate_out, up_out, product_out, branch_out):
    x = x_ref[...]
    gate = tn(jnp.concatenate([gate_own[...], gate_far[...]], axis=0), x)
    up = tn(jnp.concatenate([up_own[...], up_far[...]], axis=0), x)
    bend = jnp.tanh(GELU_SCALE * (gate + GELU_CUBE * gate * gate * gate))
    product = (0.5 * gate * (1.0 + bend) * up).astype(BF16)
    gate_out[...] = gate.astype(BF16)
    up_out[...] = up.astype(BF16)
    product_out[...] = product
    part = nn(jnp.concatenate([down_own[...], down_far[...]], axis=0), product)

    @pl.when(pl.program_id(0) == 0)
    def _():
        branch_out[...] = part

    @pl.when(pl.program_id(0) > 0)
    def _():
        branch_out[...] += part


def ffn_back_kernel(
    x_ref,
    grad_ref,
    gate_ref,
    up_ref,
    product_ref,
    gate_own,
    gate_far,
    up_own,
    up_far,
    down_own,
    down_far,
    mid_out,
    down_out,
    gate_out,
    up_out,
):
    x = x_ref[...]
    grad = grad_ref[...]
    gate = gate_ref[...].astype(F32)
    up = up_ref[...].astype(F32)
    product_grad = tn(jnp.concatenate([down_own[...], down_far[...]], axis=0), grad)
    square = gate * gate
    bend = jnp.tanh(GELU_SCALE * gate * (1.0 + GELU_CUBE * square))
    rise = 0.5 * (1.0 + bend)
    slope = rise + (0.5 * GELU_SCALE) * gate * (1.0 - bend * bend) * (1.0 + (3.0 * GELU_CUBE) * square)
    gate_grad = (product_grad * up * slope).astype(BF16)
    up_grad = (product_grad * gate * rise).astype(BF16)
    down_out[...] = nt(grad, product_ref[...]).astype(down_out.dtype)
    gate_out[...] = nt(x, gate_grad).astype(gate_out.dtype)
    up_out[...] = nt(x, up_grad).astype(up_out.dtype)
    part = nn(jnp.concatenate([gate_own[...], gate_far[...]], axis=0), gate_grad)
    part += nn(jnp.concatenate([up_own[...], up_far[...]], axis=0), up_grad)

    @pl.when(pl.program_id(0) == 0)
    def _():
        mid_out[...] = part

    @pl.when(pl.program_id(0) > 0)
    def _():
        mid_out[...] += part


def weight_specs(weights):
    specs = []
    for array, first in weights:
        specs.append(pl.BlockSpec((array.shape[0], HIDDEN), lambda i, first=first: (0, first // HIDDEN + i)))
    return specs


def ffn(x, weights, hidden):
    tokens = x.shape[1]
    rows = pl.BlockSpec((HIDDEN, tokens), lambda i: (i, 0))
    whole = pl.BlockSpec(x.shape, lambda i: (0, 0))
    wide = jax.ShapeDtypeStruct((hidden, tokens), BF16)
    return pl.pallas_call(
        ffn_kernel,
        grid=(hidden // HIDDEN,),
        in_specs=[whole] + weight_specs(weights),
        out_specs=[rows, rows, rows, whole],
        out_shape=[wide, wide, wide, jax.ShapeDtypeStruct(x.shape, F32)],
        compiler_params=pltpu.CompilerParams(vmem_limit_bytes=40 << 20),
        cost_estimate=pl.CostEstimate(
            flops=6 * hidden * tokens * D, bytes_accessed=12 * hidden * tokens, transcendentals=hidden * tokens
        ),
        name="ffn",
    )(x, *(array for array, _ in weights))


def ffn_back(x, grad, gate, up, product, weights, hidden, kind):
    tokens = x.shape[1]
    rows = pl.BlockSpec((HIDDEN, tokens), lambda i: (i, 0))
    whole = pl.BlockSpec(x.shape, lambda i: (0, 0))
    column = pl.BlockSpec((D, HIDDEN), lambda i: (0, i))
    weight = jax.ShapeDtypeStruct((D, hidden), kind)
    return pl.pallas_call(
        ffn_back_kernel,
        grid=(hidden // HIDDEN,),
        in_specs=[whole, whole, rows, rows, rows] + weight_specs(weights),
        out_specs=[whole, column, column, column],
        out_shape=[jax.ShapeDtypeStruct(x.shape, F32), weight, weight, weight],
        compiler_params=pltpu.CompilerParams(vmem_limit_bytes=40 << 20),
        cost_estimate=pl.CostEstimate(
            flops=12 * hidden * tokens * D, bytes_accessed=16 * hidden * tokens, transcendentals=hidden * tokens
        ),
        name="ffn_back",
    )(x, grad, gate, up, product, *(array for array, _ in weights))


def per_device(
    inputs,
    cotangent,
    query_weight,
    keyval_weight,
    out_weight,
    gate_weight,
    up_weight,
    down_weight,
    attend_in_gain,
    attend_out_gain,
    forward_in_gain,
    forward_out_gain,
    query_gain,
    key_gain,
):
    assert inputs.shape[0] == LEN
    row = lax.axis_index("row")
    col = lax.axis_index("col")
    part = row * 2 + col
    tokens = LEN // PARTS
    ahead = [(i, i + 1) for i in range(PARTS - 1)]
    behind = [(i + 1, i) for i in range(PARTS - 1)]
    half = HEADS * HEAD_DIM // 2
    side = (lax.axis_index("dp")) % 2

    unit = gate_weight.shape[1]

    low = to_tokens(inputs.T, part, col)
    pack = jnp.concatenate([query_weight, keyval_weight], axis=1)
    pack_other = swap(pack, "row")
    query_col = swap(query_weight, "col")
    gains = jnp.stack([attend_in_gain, attend_out_gain, forward_in_gain, forward_out_gain])
    gains = gather_gains(gains, col)
    in_gain, out_gain, mid_gain, last_gain = (gains[i][:, None] for i in range(4))
    query_gain, key_gain = query_gain[:, None], key_gain[:, None]
    cosine, sine = rope_tables(part * tokens, tokens)
    first = jnp.where(part == 0, WINDOW, 0).astype(jnp.int32).reshape(1)

    rest = jnp.concatenate([out_weight.T, gate_weight, up_weight, down_weight.T], axis=1)
    rest_col = swap(rest, "col")
    at_gate, at_up, at_down = half, half + unit, half + 2 * unit
    rest_half = half_of(rest, side, 0)
    low, out_half = pin(low, rest_half[:, :at_up])
    out_row = swap(out_half, "row")
    pack_other, up_half = pin(pack_other, rest_half[:, at_up:at_down])
    up_row = swap(up_half, "row")
    query_other = pack_other[:, :half]
    query_full = grid4(query_weight, query_col, query_other, swap(query_other, "col"))
    keyval_full = jnp.concatenate([keyval_weight, pack_other[:, half:]], axis=0)

    residual = low.astype(F32)
    scale_in = scale_of(residual)
    attend_in = (residual * scale_in * (1.0 + in_gain)).astype(BF16)
    keyval_raw = tn(keyval_full, attend_in)
    key_raw = keyval_raw[:HEAD_DIM]
    value_rows = keyval_raw[HEAD_DIM:].astype(BF16)

    def query_prep(raw, gain):
        return rotate(rms_scale(raw, gain), cosine, sine) * HEAD_DIM ** (-0.5)

    def key_prep(raw, gain):
        return rotate(rms_scale(raw, gain), cosine, sine)

    key_ready, key_pullback = jax.vjp(key_prep, key_raw, key_gain)
    key_rows = key_ready.astype(BF16)
    halo = lax.ppermute(
        jnp.concatenate([key_rows[:, tokens - WINDOW :], value_rows[:, tokens - WINDOW :]], axis=0),
        ("row", "col"),
        ahead,
    )
    query_raw = tn(query_full, attend_in).reshape(HEADS, HEAD_DIM, tokens)
    query_ready, query_pullback = jax.vjp(query_prep, query_raw, query_gain)
    query_rows = query_ready.astype(BF16).reshape(HEADS * HEAD_DIM, tokens)
    query_rows, halo, out_row, down_half = pin(query_rows, halo, out_row, rest_half[:, at_down:])
    out_there = swap_dp(out_row, 1)
    down_row = swap(down_half, "row")
    keys = jnp.concatenate([halo[:HEAD_DIM], key_rows], axis=1)
    values = jnp.concatenate([halo[HEAD_DIM:], value_rows], axis=1)
    mixed_heads = attend(first, query_rows, keys, values)
    mixed_heads, out_there, up_row, cot = pin(mixed_heads, out_there, up_row, cotangent.T)
    out_far = ordered(side, out_row, out_there, 0)
    out_far_col = swap(out_far, "col")
    up_there = swap_dp(up_row, 1)

    out_full = grid4(rest[:, :half], rest_col[:, :half], out_far[:, :half], out_far_col[:, :half])
    branch_attn = nn(out_full, mixed_heads)
    branch_attn, up_there, down_row, cot = pin(branch_attn, up_there, down_row, cot)
    down_there = swap_dp(down_row, 1)
    upstream = to_tokens(cot, part, col)
    up_far = ordered(side, up_row, up_there, 0)
    up_far_col = swap(up_far, "col")
    scale_attn = scale_of(branch_attn)
    hidden_state = residual + branch_attn * scale_attn * (1.0 + out_gain)
    scale_mid = scale_of(hidden_state)
    forward_in = (hidden_state * scale_mid * (1.0 + mid_gain)).astype(BF16)
    forward_in, down_there = pin(forward_in, down_there)
    down_far = ordered(side, down_row, down_there, 0)
    down_far_col = swap(down_far, "col")
    own = ((rest, at_gate), (out_far, at_gate), (rest, at_up), (up_far, 0), (rest, at_down), (down_far, 0))
    other = (
        (rest_col, at_gate),
        (out_far_col, at_gate),
        (rest_col, at_up),
        (up_far_col, 0),
        (rest_col, at_down),
        (down_far_col, 0),
    )
    gate_own, up_own, product_own, branch_own = ffn(forward_in, own, unit)
    forward_in, branch_own, down_far_col = pin(forward_in, branch_own, down_far_col)
    other = other[:5] + ((down_far_col, 0),)
    gate_other, up_other, product_other, branch_other = ffn(forward_in, other, unit)
    branch_ffn = branch_own + branch_other
    scale_out = scale_of(branch_ffn)
    output = (hidden_state + branch_ffn * scale_out * (1.0 + last_gain)).astype(BF16)

    branch_ffn, upstream = pin(branch_ffn, upstream)
    upstream = upstream.astype(F32)
    output_got = send_features(output, col)
    ffn_grad, last_gain_grad = norm_backward(branch_ffn, scale_out, last_gain, upstream)
    ffn_grad = ffn_grad.astype(BF16)
    mid_other, *sent1 = ffn_back(forward_in, ffn_grad, gate_other, up_other, product_other, other, unit, BF16)
    got1 = swap(jnp.stack(sent1), "col")
    mid_other, ffn_grad = pin(mid_other, ffn_grad)
    mid_own, *own1 = ffn_back(forward_in, ffn_grad, gate_own, up_own, product_own, own, unit, F32)
    mid_own, got1 = pin(mid_own, got1)
    sum1 = jnp.concatenate([own1[0] + got1[0].astype(F32), own1[1] + got1[1].astype(F32)], axis=1)
    keep1, got1_row = row_half(sum1)

    mid_grad = mid_own + mid_other
    state_part, mid_gain_grad = norm_backward(hidden_state, scale_mid, mid_gain, mid_grad)
    state_grad = upstream + state_part
    attn_grad, out_gain_grad = norm_backward(branch_attn, scale_attn, out_gain, state_grad)
    attn_grad = attn_grad.astype(BF16)
    got2 = swap(nt(attn_grad, mixed_heads[half:]).astype(BF16), "col")
    own2 = nt(attn_grad, mixed_heads[:half])
    heads_grad = tn(out_full, attn_grad).astype(BF16)
    heads_grad, got2, own2 = pin(heads_grad, got2, own2)
    sum2 = jnp.concatenate([own1[2] + got1[2].astype(F32), own2 + got2.astype(F32)], axis=1)
    keep2, got2 = dp_half(sum2)

    query_back, key_back, value_back = attend_back(first, query_rows, keys, values, heads_grad)
    back = lax.ppermute(
        jnp.concatenate([key_back[:, :WINDOW], value_back[:, :WINDOW]], axis=0).astype(BF16),
        ("row", "col"),
        behind,
    )
    query_raw_grad, query_gain_grad = query_pullback(query_back.reshape(HEADS, HEAD_DIM, tokens))
    query_raw_grad = query_raw_grad.reshape(HEADS * HEAD_DIM, tokens).astype(BF16)
    in_query = nn(query_full, query_raw_grad)
    in_query, back, got1_row, got2 = pin(in_query, back, got1_row, got2)
    keep1, got1_dp = dp_half(keep1 + got1_row.astype(F32))
    keep2, got2_row = row_half(keep2 + got2.astype(F32))

    spare = tokens - WINDOW
    back = jnp.pad(back.astype(F32), ((0, 0), (spare, 0)))
    key_raw_grad, key_gain_grad = key_pullback(key_back[:, WINDOW:] + back[:HEAD_DIM])
    value_grad = value_back[:, WINDOW:] + back[HEAD_DIM:]
    keyval_raw_grad = jnp.concatenate([key_raw_grad, value_grad], axis=0).astype(BF16)
    in_grad = in_query + nn(keyval_full, keyval_raw_grad)
    residual_part, in_gain_grad = norm_backward(residual, scale_in, in_gain, in_grad)

    pad = jnp.zeros((D // 2 - HEAD_DIM, 2), F32)
    heads_gain_grad = jnp.concatenate([query_gain_grad, key_gain_grad], axis=1)
    gain_grads = jnp.concatenate(
        [
            in_gain_grad,
            out_gain_grad,
            mid_gain_grad,
            last_gain_grad,
            jnp.concatenate([heads_gain_grad, pad, heads_gain_grad, pad], axis=0),
            jnp.zeros((D, 122), F32),
        ],
        axis=1,
    )
    own3 = jnp.concatenate(
        [nt(attend_in, query_raw_grad[:half]), nt(attend_in, half_of(keyval_raw_grad, col, 0)), gain_grads], axis=1
    )
    sent3 = jnp.concatenate(
        [nt(attend_in, query_raw_grad[half:]), nt(attend_in, half_of(keyval_raw_grad, 1 - col, 0)), gain_grads], axis=1
    ).astype(BF16)
    got3 = swap(sent3, "col")
    input_grad = (state_grad + residual_part).astype(BF16)
    own3, got3, got1_dp, input_grad = pin(own3, got3, got1_dp, input_grad)
    keep3, got3 = row_half(own3 + got3.astype(F32))
    shares1 = spread(keep1 + got1_dp.astype(F32), 2)
    got3, got2_row, input_grad = pin(got3, got2_row, input_grad)
    shares3 = spread(keep3 + got3.astype(F32), 1)
    input_got = send_features(input_grad, col)
    shares2 = spread(keep2 + got2_row.astype(F32), 2)
    whole1 = dp_whole(collect(shares1, 2))
    whole3 = collect(shares3, 1)
    whole2 = dp_whole(collect(shares2, 2))

    keyval_mine = whole3[:, half : half + HEAD_DIM]
    keyval_grad = ordered(col, keyval_mine, swap(keyval_mine, "col"), 1)
    gain_all = whole3[:, half + HEAD_DIM :].astype(F32)
    gain_mine = half_of(gain_all, col, 0)
    output = join_features(output_got, part)
    input_grad = join_features(input_got, part)
    return (
        output.T,
        input_grad.T.astype(F32),
        whole3[:, :half].astype(F32),
        keyval_grad.astype(F32),
        whole2[:, unit:].T.astype(F32),
        whole1[:, unit:].astype(F32),
        whole2[:, :unit].astype(F32),
        whole1[:, :unit].T.astype(F32),
        gain_mine[:, 0],
        gain_mine[:, 1],
        gain_mine[:, 2],
        gain_mine[:, 3],
        gain_all[:HEAD_DIM, 4],
        gain_all[:HEAD_DIM, 5],
    )


def solution(mesh):
    wide = P("dp", ("row", "col"))
    gain = P(("row", "col"))
    weights = (P("row", "col"), P("row", None), P("col", "row"), P("row", "col"), P("row", "col"), P("col", "row"))
    gains = (gain, gain, gain, gain, P(), P())
    return jax.shard_map(
        per_device,
        mesh=mesh,
        in_specs=(wide, wide) + weights + gains,
        out_specs=(wide, wide) + weights + gains,
        check_vma=False,
    )
```

```python
import jax
import jax.numpy as jnp
from jax import lax
from jax.experimental import pallas as pl
from jax.experimental.pallas import tpu as pltpu
from jax.sharding import PartitionSpec as P

D = 640
HEADS = 4
HEAD_DIM = 256
WINDOW = 512
LEN = 4096
PARTS = 4
BLOCK = 256
SPAN = BLOCK + WINDOW

EPSILON = 1e-06
ROPE_BASE = 10000.0

F32 = jnp.float32
SLOW = pl.CostEstimate(flops=60_000_000_000, bytes_accessed=100_000_000, transcendentals=0)
QUICK = pl.CostEstimate(flops=1000, bytes_accessed=1000, transcendentals=0)
BF16 = jnp.bfloat16


def pin(*values):
    return lax.optimization_barrier(values)


def swap(values, axis):
    return lax.ppermute(values, axis, [(0, 1), (1, 0)])


def swap_dp(values, bit):
    size = lax.axis_size("dp")
    return lax.ppermute(values, "dp", [(i, i ^ bit) for i in range(size)])


def swap_part(values, k):
    return lax.ppermute(values, ("row", "col"), [(i, i ^ k) for i in range(PARTS)])


def ordered(flag, own, other, axis):
    first = jnp.where(flag == 0, own, other)
    second = jnp.where(flag == 0, other, own)
    return jnp.concatenate([first, second], axis=axis)


def half_of(values, index, axis):
    length = values.shape[axis] // 2
    return lax.dynamic_slice_in_dim(values, index * length, length, axis)


def to_tokens(values, part, col):
    tokens = values.shape[1] // PARTS

    def block(k):
        return lax.dynamic_slice_in_dim(values, (part ^ k) * tokens, tokens, 1)

    got = [block(0)] + [swap_part(block(k), k) for k in (1, 2, 3)]
    return jnp.concatenate(
        [ordered(col, got[0], got[1], 0), ordered(col, got[2], got[3], 0)], axis=0
    )


def send_features(values, col):
    width = values.shape[0] // PARTS
    quarters = [values[i * width : (i + 1) * width] for i in range(PARTS)]
    sent = []
    for pair in (quarters[:2], quarters[2:]):
        sent.append(jnp.where(col == 0, pair[0], pair[1]))
        sent.append(jnp.where(col == 0, pair[1], pair[0]))
    return [sent[0]] + [swap_part(sent[k], k) for k in (1, 2, 3)]


def join_features(got, part):
    out = []
    for block in range(PARTS):
        piece = got[0]
        for k in (1, 2, 3):
            piece = jnp.where((part ^ k) == block, got[k], piece)
        out.append(piece)
    return jnp.concatenate(out, axis=1)


def gather_gains(gains, col):
    half = ordered(col, gains, swap(gains, "col"), 1)
    return jnp.concatenate([half, swap(half, "row")], axis=1)


def grid4(own, own_col, other, other_col):
    return jnp.concatenate(
        [jnp.concatenate([own, own_col], axis=1), jnp.concatenate([other, other_col], axis=1)], axis=0
    )


def dp_bits():
    bits, bit = [], 1
    while bit < lax.axis_size("dp"):
        bits.append(bit)
        bit *= 2
    return bits


def bit_of(bit):
    return (lax.axis_index("dp") // bit) % 2


def dp_half(total, bit, axis=1):
    mine = bit_of(bit)
    return half_of(total, mine, axis), swap_dp(half_of(total, 1 - mine, axis).astype(BF16), bit)


def dp_back(values, bit, axis=1):
    return ordered(bit_of(bit), values, swap_dp(values, bit), axis)


def plus(keep, got):
    return keep.astype(F32) + got.astype(F32)


def row_half(total):
    rows = total.shape[0] // 2
    return total[:rows], swap(total[rows:].astype(BF16), "row")


def spread(total):
    count = lax.axis_size("dp")
    rows, cols = total.shape
    shares = total.astype(BF16).reshape(count, rows // count, cols)
    return lax.all_to_all(shares, "dp", 0, 0, tiled=True)


def collect(shares):
    count, rows, cols = shares.shape
    share = jnp.sum(shares.astype(F32), axis=0, keepdims=True).astype(BF16)
    whole = lax.all_to_all(jnp.broadcast_to(share, shares.shape), "dp", 0, 0, tiled=True)
    return whole.reshape(count * rows, cols)


def scale_of(values):
    return lax.rsqrt(jnp.mean(values * values, axis=-2, keepdims=True) + EPSILON)


def norm_backward(values, scale, offset, gradient):
    unit = values * scale
    scaled = gradient * (1.0 + offset)
    inner = jnp.mean(scaled * unit, axis=0, keepdims=True)
    return scale * (scaled - unit * inner), jnp.sum(gradient * unit, axis=1)


def rms_scale(values, offset):
    return values * scale_of(values) * (1.0 + offset)


def rotate(values, cosine, sine):
    half_dim = values.shape[-2] // 2
    first_half = values[..., :half_dim, :]
    second_half = values[..., half_dim:, :]
    return jnp.concatenate(
        [first_half * cosine - second_half * sine, second_half * cosine + first_half * sine],
        axis=-2,
    )


def rope_tables(first, count):
    half_dim = HEAD_DIM // 2
    frequency = ROPE_BASE ** (-(jnp.arange(half_dim, dtype=F32) * 2.0 / HEAD_DIM))
    angles = (first + jnp.arange(count, dtype=jnp.int32)).astype(F32)[None, :] * frequency[:, None]
    return (jnp.cos(angles), jnp.sin(angles))


def nn(a, b):
    return jnp.dot(a, b, preferred_element_type=F32)


def nt(a, b):
    return lax.dot_general(a, b, (((1,), (1,)), ((), ())), preferred_element_type=F32)


def tn(a, b):
    return lax.dot_general(a, b, (((0,), (0,)), ((), ())), preferred_element_type=F32)


def seen_mask(first_key):
    key = lax.broadcasted_iota(jnp.int32, (SPAN, BLOCK), 0)
    query = lax.broadcasted_iota(jnp.int32, (SPAN, BLOCK), 1)
    return (key > query) & (key <= query + WINDOW) & (key >= first_key)


def attend_kernel(first_ref, query_ref, key_ref, value_ref, out_ref):
    start = pl.multiple_of(pl.program_id(0) * BLOCK, BLOCK)
    keys = key_ref[:, pl.ds(start, SPAN)].T
    values = value_ref[:, pl.ds(start, SPAN)]
    mask = seen_mask(first_ref[0] - start)
    for head in range(HEADS):
        features = slice(head * HEAD_DIM, (head + 1) * HEAD_DIM)
        weights = jnp.where(mask, jnp.exp(nn(keys, query_ref[features, :])), 0.0)
        total = jnp.sum(weights, axis=0, keepdims=True)
        probs = (weights * (1.0 / total)).astype(BF16)
        out_ref[features, :] = nn(values, probs).astype(BF16)


def attend_back_kernel(first_ref, query_ref, key_ref, value_ref, grad_ref, query_out, key_out, value_out):
    block = pl.program_id(0)
    start = pl.multiple_of(block * BLOCK, BLOCK)
    window = pl.ds(start, SPAN)
    keys_wide = key_ref[:, window]
    keys = keys_wide.T
    values = value_ref[:, window].T
    mask = seen_mask(first_ref[0] - start)

    @pl.when(block == 0)
    def _():
        key_out[...] = jnp.zeros_like(key_out)
        value_out[...] = jnp.zeros_like(value_out)

    key_sum = key_out[:, window]
    value_sum = value_out[:, window]
    for head in range(HEADS):
        features = slice(head * HEAD_DIM, (head + 1) * HEAD_DIM)
        queries = query_ref[features, :]
        grads = grad_ref[features, :]
        weights = jnp.where(mask, jnp.exp(nn(keys, queries)), 0.0)
        probs = weights * (1.0 / jnp.sum(weights, axis=0, keepdims=True))
        prob_grad = nn(values, grads)
        inner = jnp.sum(prob_grad * probs, axis=0, keepdims=True)
        score_grad = (probs * (prob_grad - inner)).astype(BF16)
        query_out[features, :] = nn(keys_wide, score_grad)
        key_sum += nt(queries, score_grad)
        value_sum += nt(grads, probs.astype(BF16))
    key_out[:, window] = key_sum
    value_out[:, window] = value_sum


def attend_call(kernel, name, out_specs, out_shape, products, arrays):
    width, tokens = arrays[1].shape
    span = arrays[2].shape[1]
    block = pl.BlockSpec((width, BLOCK), lambda i: (0, i))
    whole = pl.BlockSpec((HEAD_DIM, span), lambda i: (0, 0))
    return pl.pallas_call(
        kernel,
        grid=(tokens // BLOCK,),
        in_specs=[pl.BlockSpec(memory_space=pltpu.SMEM), block, whole, whole] + [block] * (len(arrays) - 4),
        out_specs=[{"block": block, "whole": whole}[spec] for spec in out_specs],
        out_shape=out_shape,
        compiler_params=pltpu.CompilerParams(vmem_limit_bytes=20 << 20),
        cost_estimate=QUICK,
        name=name,
    )(*arrays)


def attend(first, queries, keys, values):
    shape = [jax.ShapeDtypeStruct(queries.shape, BF16)]
    return attend_call(attend_kernel, "attend", ["block"], shape, 2, (first, queries, keys, values))[0]


def attend_back(first, queries, keys, values, heads_grad):
    shapes = [jax.ShapeDtypeStruct(a.shape, F32) for a in (queries, keys, values)]
    return attend_call(
        attend_back_kernel,
        "attend_back",
        ["block", "whole", "whole"],
        shapes,
        5,
        (first, queries, keys, values, heads_grad),
    )


HIDDEN = 256
LANES = 128
GELU_SCALE = 0.7978845608028654
GELU_CUBE = 0.044715


def ffn_kernel(x_ref, gate_own, gate_far, up_own, up_far, down_own, down_far, gate_out, up_out, product_out, branch_out):
    x = x_ref[...]
    gate = tn(jnp.concatenate([gate_own[...], gate_far[...]], axis=0), x)
    up = tn(jnp.concatenate([up_own[...], up_far[...]], axis=0), x)
    bend = jnp.tanh(GELU_SCALE * (gate + GELU_CUBE * gate * gate * gate))
    product = (0.5 * gate * (1.0 + bend) * up).astype(BF16)
    gate_out[...] = gate.astype(BF16)
    up_out[...] = up.astype(BF16)
    product_out[...] = product
    part = nn(jnp.concatenate([down_own[...], down_far[...]], axis=0), product)

    @pl.when(pl.program_id(0) == 0)
    def _():
        branch_out[...] = part

    @pl.when(pl.program_id(0) > 0)
    def _():
        branch_out[...] += part


def ffn_back_kernel(
    x_ref,
    grad_ref,
    gate_ref,
    up_ref,
    product_ref,
    gate_own,
    gate_far,
    up_own,
    up_far,
    down_own,
    down_far,
    mid_out,
    weight_out,
):
    x = x_ref[...]
    grad = grad_ref[...]
    gate = gate_ref[...].astype(F32)
    up = up_ref[...].astype(F32)
    product_grad = tn(jnp.concatenate([down_own[...], down_far[...]], axis=0), grad)
    square = gate * gate
    bend = jnp.tanh(GELU_SCALE * gate * (1.0 + GELU_CUBE * square))
    rise = 0.5 * (1.0 + bend)
    slope = rise + (0.5 * GELU_SCALE) * gate * (1.0 - bend * bend) * (1.0 + (3.0 * GELU_CUBE) * square)
    gate_grad = (product_grad * up * slope).astype(BF16)
    up_grad = (product_grad * gate * rise).astype(BF16)
    kind = weight_out.dtype
    weight_out[0] = nt(grad, product_ref[...]).astype(kind)
    weight_out[1] = nt(x, gate_grad).astype(kind)
    weight_out[2] = nt(x, up_grad).astype(kind)
    part = nn(jnp.concatenate([gate_own[...], gate_far[...]], axis=0), gate_grad)
    part += nn(jnp.concatenate([up_own[...], up_far[...]], axis=0), up_grad)

    @pl.when(pl.program_id(0) == 0)
    def _():
        mid_out[...] = part

    @pl.when(pl.program_id(0) > 0)
    def _():
        mid_out[...] += part


def attend_weights_kernel(col_ref, x_ref, query_ref, keyval_ref, gain_ref, own_out, sent_out):
    x = x_ref[...]
    half = query_ref.shape[0] // 2
    col = col_ref[0]
    wide = jnp.concatenate([gain_ref[...], jnp.zeros((LANES - gain_ref.shape[0], D), F32)], axis=0)
    gains = wide.T
    for out, start, which in ((sent_out, half, 1 - col), (own_out, 0, col)):
        rows = pl.ds(pl.multiple_of(which * HEAD_DIM, HEAD_DIM), HEAD_DIM)
        out[:, :half] = nt(x, query_ref[start : start + half, :]).astype(out.dtype)
        out[:, half : half + HEAD_DIM] = nt(x, keyval_ref[rows, :]).astype(out.dtype)
        out[:, half + HEAD_DIM :] = gains.astype(out.dtype)


def attend_weights(col, x, query_grad, keyval_grad, gain_grads):
    width = query_grad.shape[0] // 2 + HEAD_DIM + LANES
    vmem = pl.BlockSpec(memory_space=pltpu.VMEM)
    return pl.pallas_call(
        attend_weights_kernel,
        in_specs=[pl.BlockSpec(memory_space=pltpu.SMEM), vmem, vmem, vmem, vmem],
        out_specs=[vmem, vmem],
        out_shape=[jax.ShapeDtypeStruct((D, width), F32), jax.ShapeDtypeStruct((D, width), BF16)],
        compiler_params=pltpu.CompilerParams(vmem_limit_bytes=24 << 20),
        cost_estimate=QUICK,
        name="attend_weights",
    )(col.astype(jnp.int32).reshape(1), x, query_grad, keyval_grad, gain_grads)


def far(values):
    return pltpu.with_memory_space_constraint(values, pltpu.HBM)


def weight_specs(weights):
    specs = []
    for array, first in weights:
        specs.append(pl.BlockSpec((array.shape[0], HIDDEN), lambda i, first=first: (0, first // HIDDEN + i)))
    return specs


def ffn(x, weights, hidden):
    tokens = x.shape[1]
    rows = pl.BlockSpec((HIDDEN, tokens), lambda i: (i, 0))
    whole = pl.BlockSpec(x.shape, lambda i: (0, 0))
    once = pl.BlockSpec(x.shape, lambda i: (0, 0), pipeline_mode=pl.Buffered(1))
    wide = pltpu.HBM((hidden, tokens), BF16)
    return pl.pallas_call(
        ffn_kernel,
        grid=(hidden // HIDDEN,),
        in_specs=[once] + weight_specs(weights),
        out_specs=[rows, rows, rows, whole],
        out_shape=[wide, wide, wide, jax.ShapeDtypeStruct(x.shape, F32)],
        compiler_params=pltpu.CompilerParams(vmem_limit_bytes=24 << 20),
        cost_estimate=SLOW,
        name="ffn",
    )(x, *(far(array) for array, _ in weights))


def ffn_back(x, grad, gate, up, product, weights, hidden, kind):
    tokens = x.shape[1]
    rows = pl.BlockSpec((HIDDEN, tokens), lambda i: (i, 0))
    whole = pl.BlockSpec(x.shape, lambda i: (0, 0))
    once = pl.BlockSpec(x.shape, lambda i: (0, 0), pipeline_mode=pl.Buffered(1))
    column = pl.BlockSpec((3, D, HIDDEN), lambda i: (0, 0, i))
    weight = pltpu.HBM((3, D, hidden), kind)
    return pl.pallas_call(
        ffn_back_kernel,
        grid=(hidden // HIDDEN,),
        in_specs=[once, once, rows, rows, rows] + weight_specs(weights),
        out_specs=[whole, column],
        out_shape=[jax.ShapeDtypeStruct(x.shape, F32), weight],
        compiler_params=pltpu.CompilerParams(vmem_limit_bytes=28 << 20),
        cost_estimate=SLOW,
        name="ffn_back",
    )(*(far(array) for array in (x, grad, gate, up, product)), *(far(array) for array, _ in weights))


def per_device(
    inputs,
    cotangent,
    query_weight,
    keyval_weight,
    out_weight,
    gate_weight,
    up_weight,
    down_weight,
    attend_in_gain,
    attend_out_gain,
    forward_in_gain,
    forward_out_gain,
    query_gain,
    key_gain,
):
    assert inputs.shape[0] == LEN
    row = lax.axis_index("row")
    col = lax.axis_index("col")
    part = row * 2 + col
    tokens = LEN // PARTS
    ahead = [(i, i + 1) for i in range(PARTS - 1)]
    behind = [(i + 1, i) for i in range(PARTS - 1)]
    half = HEADS * HEAD_DIM // 2

    unit = gate_weight.shape[1]

    low = to_tokens(inputs.T, part, col)
    pack = jnp.concatenate([query_weight, keyval_weight], axis=1)
    pack_other = swap(pack, "row")
    query_col = swap(query_weight, "col")
    gains = jnp.stack([attend_in_gain, attend_out_gain, forward_in_gain, forward_out_gain])
    gains = gather_gains(gains, col)
    in_gain, out_gain, mid_gain, last_gain = (gains[i][:, None] for i in range(4))
    query_gain, key_gain = query_gain[:, None], key_gain[:, None]
    cosine, sine = rope_tables(part * tokens, tokens)
    first = jnp.where(part == 0, WINDOW, 0).astype(jnp.int32).reshape(1)

    rest = jnp.concatenate([out_weight.T, gate_weight, up_weight, down_weight.T], axis=1)
    rest_col = swap(rest, "col")
    at_gate, at_up, at_down = half, half + unit, half + 2 * unit
    rest_half = half_of(rest[:, :at_down], bit_of(1), 0)
    low, out_half = pin(low, rest_half[:, :at_up])
    out_row = swap(out_half, "row")
    pack_other, up_half = pin(pack_other, rest_half[:, at_up:at_down])
    up_row = swap(up_half, "row")
    query_other = pack_other[:, :half]
    query_full = grid4(query_weight, query_col, query_other, swap(query_other, "col"))
    keyval_full = jnp.concatenate([keyval_weight, pack_other[:, half:]], axis=0)

    residual = low.astype(F32)
    scale_in = scale_of(residual)
    attend_in = (residual * scale_in * (1.0 + in_gain)).astype(BF16)
    keyval_raw = tn(keyval_full, attend_in)
    key_raw = keyval_raw[:HEAD_DIM]
    value_rows = keyval_raw[HEAD_DIM:].astype(BF16)

    def query_prep(raw, gain):
        return rotate(rms_scale(raw, gain), cosine, sine) * HEAD_DIM ** (-0.5)

    def key_prep(raw, gain):
        return rotate(rms_scale(raw, gain), cosine, sine)

    key_ready, key_pullback = jax.vjp(key_prep, key_raw, key_gain)
    key_rows = key_ready.astype(BF16)
    halo = lax.ppermute(
        jnp.concatenate([key_rows[:, tokens - WINDOW :], value_rows[:, tokens - WINDOW :]], axis=0),
        ("row", "col"),
        ahead,
    )
    query_raw = tn(query_full, attend_in).reshape(HEADS, HEAD_DIM, tokens)
    query_ready, query_pullback = jax.vjp(query_prep, query_raw, query_gain)
    query_rows = query_ready.astype(BF16).reshape(HEADS * HEAD_DIM, tokens)
    query_rows, halo, out_row, down_half = pin(query_rows, halo, out_row, half_of(rest[:, at_down:], bit_of(2), 0))
    out_there = swap_dp(out_row, 1)
    down_row = swap(down_half, "row")
    keys = jnp.concatenate([halo[:HEAD_DIM], key_rows], axis=1)
    values = jnp.concatenate([halo[HEAD_DIM:], value_rows], axis=1)
    mixed_heads = attend(first, query_rows, keys, values)
    mixed_heads, out_there, up_row, cot = pin(mixed_heads, out_there, up_row, cotangent.T)
    out_far = ordered(bit_of(1), out_row, out_there, 0)
    out_far_col = swap(out_far, "col")
    up_there = swap_dp(up_row, 1)

    out_full = grid4(rest[:, :half], rest_col[:, :half], out_far[:, :half], out_far_col[:, :half])
    branch_attn = nn(out_full, mixed_heads)
    branch_attn, up_there, down_row, cot = pin(branch_attn, up_there, down_row, cot)
    down_there = swap_dp(down_row, 2)
    upstream = to_tokens(cot, part, col)
    up_far = ordered(bit_of(1), up_row, up_there, 0)
    up_far_col = swap(up_far, "col")
    scale_attn = scale_of(branch_attn)
    hidden_state = residual + branch_attn * scale_attn * (1.0 + out_gain)
    scale_mid = scale_of(hidden_state)
    forward_in = (hidden_state * scale_mid * (1.0 + mid_gain)).astype(BF16)
    forward_in, down_there = pin(forward_in, down_there)
    down_far = ordered(bit_of(2), down_row, down_there, 0)
    down_far_col = swap(down_far, "col")
    own = ((rest, at_gate), (out_far, at_gate), (rest, at_up), (up_far, 0), (rest, at_down), (down_far, 0))
    other = (
        (rest_col, at_gate),
        (out_far_col, at_gate),
        (rest_col, at_up),
        (up_far_col, 0),
        (rest_col, at_down),
        (down_far_col, 0),
    )
    gate_own, up_own, product_own, branch_own = ffn(forward_in, own, unit)
    forward_in, branch_own, down_far_col = pin(forward_in, branch_own, down_far_col)
    other = other[:5] + ((down_far_col, 0),)
    gate_other, up_other, product_other, branch_other = ffn(forward_in, other, unit)
    branch_ffn = branch_own + branch_other
    scale_out = scale_of(branch_ffn)
    output = (hidden_state + branch_ffn * scale_out * (1.0 + last_gain)).astype(BF16)

    branch_ffn, upstream = pin(branch_ffn, upstream)
    upstream = upstream.astype(F32)
    output_got = send_features(output, col)
    ffn_grad, last_gain_grad = norm_backward(branch_ffn, scale_out, last_gain, upstream)
    ffn_grad = ffn_grad.astype(BF16)
    mid_other, sent1 = ffn_back(forward_in, ffn_grad, gate_other, up_other, product_other, other, unit, BF16)
    got1 = swap(sent1, "col")
    mid_other, ffn_grad, *output_got = pin(mid_other, ffn_grad, *output_got)
    mid_own, own1 = ffn_back(forward_in, ffn_grad, gate_own, up_own, product_own, own, unit, BF16)
    mid_own, got1 = pin(mid_own, got1)
    low_gate, high_gate = own1[1][:, : unit // 2], own1[1][:, unit // 2 :]
    low_got, high_got = got1[1][:, : unit // 2], got1[1][:, unit // 2 :]
    keep1, got1_a = row_half(jnp.concatenate([plus(own1[0], got1[0]), plus(low_gate, low_got)], axis=1))
    keep2, got2_a = dp_half(jnp.concatenate([plus(high_gate, high_got), plus(own1[2], got1[2])], axis=1), 2)

    mid_grad = mid_own + mid_other
    state_part, mid_gain_grad = norm_backward(hidden_state, scale_mid, mid_gain, mid_grad)
    state_grad = upstream + state_part
    attn_grad, out_gain_grad = norm_backward(branch_attn, scale_attn, out_gain, state_grad)
    attn_grad = attn_grad.astype(BF16)
    got_out = swap(nt(attn_grad, mixed_heads[half:]).astype(BF16), "col")
    own_out = nt(attn_grad, mixed_heads[:half])
    heads_grad = tn(out_full, attn_grad).astype(BF16)

    query_back, key_back, value_back = attend_back(first, query_rows, keys, values, heads_grad)
    back = lax.ppermute(
        jnp.concatenate([key_back[:, :WINDOW], value_back[:, :WINDOW]], axis=0).astype(BF16),
        ("row", "col"),
        behind,
    )
    query_back, got_out, own_out, got1_a, got2_a = pin(query_back, got_out, own_out, got1_a, got2_a)
    keep1, got1_b = dp_half(plus(keep1, got1_a), 1)
    keep2, got2_b = row_half(plus(keep2, got2_a))
    keep_out, got_out = row_half(plus(own_out, got_out))
    query_raw_grad, query_gain_grad = query_pullback(query_back.reshape(HEADS, HEAD_DIM, tokens))
    query_raw_grad = query_raw_grad.reshape(HEADS * HEAD_DIM, tokens).astype(BF16)
    in_query = nn(query_full, query_raw_grad)
    in_query, back, got1_b, got2_b, got_out = pin(in_query, back, got1_b, got2_b, got_out)
    keep1, got1_c = dp_half(plus(keep1, got1_b), 2)
    keep2, keep_out = plus(keep2, got2_b), plus(keep_out, got_out)
    width2, width_out = keep2.shape[1] // 2, half // 2
    keep2, got2_c = dp_half(
        jnp.concatenate(
            [keep2[:, :width2], keep_out[:, :width_out], keep2[:, width2:], keep_out[:, width_out:]], axis=1
        ),
        1,
    )
    spare = tokens - WINDOW
    back = jnp.pad(back.astype(F32), ((0, 0), (spare, 0)))
    key_raw_grad, key_gain_grad = key_pullback(key_back[:, WINDOW:] + back[:HEAD_DIM])
    value_grad = value_back[:, WINDOW:] + back[HEAD_DIM:]
    keyval_raw_grad = jnp.concatenate([key_raw_grad, value_grad], axis=0).astype(BF16)
    in_grad = in_query + nn(keyval_full, keyval_raw_grad)
    residual_part, in_gain_grad = norm_backward(residual, scale_in, in_gain, in_grad)

    pad = jnp.zeros((D // 2 - HEAD_DIM,), F32)
    query_gain_grad, key_gain_grad = query_gain_grad[:, 0], key_gain_grad[:, 0]
    gain_grads = jnp.stack(
        [
            in_gain_grad,
            out_gain_grad,
            mid_gain_grad,
            last_gain_grad,
            jnp.concatenate([query_gain_grad, pad, query_gain_grad, pad]),
            jnp.concatenate([key_gain_grad, pad, key_gain_grad, pad]),
            jnp.zeros((D,), F32),
            jnp.zeros((D,), F32),
        ]
    )
    input_grad = (state_grad + residual_part).astype(BF16)
    own3, sent3 = attend_weights(col, attend_in, query_raw_grad, keyval_raw_grad, gain_grads)
    got3 = swap(sent3, "col")
    own3, got3, got1_c, got2_c = pin(own3, got3, got1_c, got2_c)
    keep3, got3 = row_half(plus(own3, got3))
    keep1, keep2 = plus(keep1, got1_c), plus(keep2, got2_c)
    width1 = keep1.shape[1]
    keep12 = jnp.concatenate([keep1, keep2[:, :width2]], axis=1)
    share_out = keep2[:, width2:].astype(BF16)
    there_out = swap_dp(share_out, 2)
    bits = dp_bits()[2:]
    for bit in bits[:-1]:
        keep12 = plus(*dp_half(keep12, bit, 0))
    if bits:
        keep12, got12 = dp_half(keep12, bits[-1], 0)

    got3, got12, there_out, input_grad = pin(got3, got12, there_out, input_grad)
    shares3 = spread(plus(keep3, got3))
    input_got = send_features(input_grad, col)
    half12 = plus(keep12, got12).astype(BF16)
    for bit in reversed(bits):
        half12 = dp_back(half12, bit, 0)
    for bit in bits:
        share_out = plus(share_out.astype(F32), there_out).astype(BF16)
        there_out = swap_dp(share_out, bit)
    share_out = plus(share_out.astype(F32), there_out).astype(BF16)
    half12, share_out = pin(half12, share_out)
    half1, half2 = half12[:, :width1], jnp.concatenate([half12[:, width1:], share_out], axis=1)
    there1, there2 = swap_dp(half1, 2), swap_dp(half2, 1)
    whole1 = ordered(bit_of(2), half1, there1, 1)
    whole2 = ordered(bit_of(1), half2[:, :width2], there2[:, :width2], 1)
    whole_out = ordered(bit_of(1), half2[:, width2:], there2[:, width2:], 1)
    there1, there2 = swap_dp(whole1, 1), swap_dp(whole2, 2)
    shares3, *input_got = pin(shares3, *input_got)
    whole3 = collect(shares3)
    whole1 = ordered(bit_of(1), whole1, there1, 1)
    whole2 = ordered(bit_of(2), whole2, there2, 1)
    down_grad, gate_low = whole1[:, :unit], whole1[:, unit:]
    gate_high, up_grad = whole2[:, : unit // 2], whole2[:, unit // 2 :]
    gate_grad = jnp.concatenate([gate_low, gate_high], axis=1)

    keyval_mine = whole3[:, half : half + HEAD_DIM]
    keyval_grad = ordered(col, keyval_mine, swap(keyval_mine, "col"), 1)
    gain_all = whole3[:, half + HEAD_DIM :].astype(F32)
    gain_mine = half_of(gain_all, col, 0)
    output = join_features(output_got, part)
    input_grad = join_features(input_got, part)
    return (
        output.T,
        input_grad.T.astype(F32),
        whole3[:, :half].astype(F32),
        keyval_grad.astype(F32),
        whole_out.T.astype(F32),
        gate_grad.astype(F32),
        up_grad.astype(F32),
        down_grad.T.astype(F32),
        gain_mine[:, 0],
        gain_mine[:, 1],
        gain_mine[:, 2],
        gain_mine[:, 3],
        gain_all[:HEAD_DIM, 4],
        gain_all[:HEAD_DIM, 5],
    )


def solution(mesh):
    wide = P("dp", ("row", "col"))
    gain = P(("row", "col"))
    weights = (P("row", "col"), P("row", None), P("col", "row"), P("row", "col"), P("row", "col"), P("col", "row"))
    gains = (gain, gain, gain, gain, P(), P())
    return jax.shard_map(
        per_device,
        mesh=mesh,
        in_specs=(wide, wide) + weights + gains,
        out_specs=(wide, wide) + weights + gains,
        check_vma=False,
    )
```

```python
import jax
import jax.numpy as jnp
from jax import lax
from jax.experimental import pallas as pl
from jax.experimental.pallas import tpu as pltpu
from jax.sharding import PartitionSpec as P

D = 640
HEADS = 4
HEAD_DIM = 256
WINDOW = 512
LEN = 4096
PARTS = 4
BLOCK = 256
SPAN = BLOCK + WINDOW

EPSILON = 1e-06
ROPE_BASE = 10000.0

F32 = jnp.float32
SLOW = pl.CostEstimate(flops=60_000_000_000, bytes_accessed=100_000_000, transcendentals=0)
QUICK = pl.CostEstimate(flops=1000, bytes_accessed=1000, transcendentals=0)
BF16 = jnp.bfloat16


def pin(*values):
    return lax.optimization_barrier(values)


def swap(values, axis):
    return lax.ppermute(values, axis, [(0, 1), (1, 0)])


def swap_dp(values, bit):
    size = lax.axis_size("dp")
    return lax.ppermute(values, "dp", [(i, i ^ bit) for i in range(size)])


def swap_part(values, k):
    return lax.ppermute(values, ("row", "col"), [(i, i ^ k) for i in range(PARTS)])


def ordered(flag, own, other, axis):
    first = jnp.where(flag == 0, own, other)
    second = jnp.where(flag == 0, other, own)
    return jnp.concatenate([first, second], axis=axis)


def half_of(values, index, axis):
    length = values.shape[axis] // 2
    return lax.dynamic_slice_in_dim(values, index * length, length, axis)


def to_tokens(values, part, col):
    tokens = values.shape[1] // PARTS

    def block(k):
        return lax.dynamic_slice_in_dim(values, (part ^ k) * tokens, tokens, 1)

    got = [block(0)] + [swap_part(block(k), k) for k in (1, 2, 3)]
    return jnp.concatenate(
        [ordered(col, got[0], got[1], 0), ordered(col, got[2], got[3], 0)], axis=0
    )


def send_features(values, col):
    width = values.shape[0] // PARTS
    quarters = [values[i * width : (i + 1) * width] for i in range(PARTS)]
    sent = []
    for pair in (quarters[:2], quarters[2:]):
        sent.append(jnp.where(col == 0, pair[0], pair[1]))
        sent.append(jnp.where(col == 0, pair[1], pair[0]))
    return [sent[0]] + [swap_part(sent[k], k) for k in (1, 2, 3)]


def join_features(got, part):
    out = []
    for block in range(PARTS):
        piece = got[0]
        for k in (1, 2, 3):
            piece = jnp.where((part ^ k) == block, got[k], piece)
        out.append(piece)
    return jnp.concatenate(out, axis=1)


def gather_gains(gains, col):
    half = ordered(col, gains, swap(gains, "col"), 1)
    return jnp.concatenate([half, swap(half, "row")], axis=1)


def grid4(own, own_col, other, other_col):
    return jnp.concatenate(
        [jnp.concatenate([own, own_col], axis=1), jnp.concatenate([other, other_col], axis=1)], axis=0
    )


def dp_bits():
    bits, bit = [], 1
    while bit < lax.axis_size("dp"):
        bits.append(bit)
        bit *= 2
    return bits


def bit_of(bit):
    return (lax.axis_index("dp") // bit) % 2


def dp_half(total, bit, axis=1):
    mine = bit_of(bit)
    return half_of(total, mine, axis), swap_dp(half_of(total, 1 - mine, axis).astype(BF16), bit)


def dp_back(values, bit, axis=1):
    return ordered(bit_of(bit), values, swap_dp(values, bit), axis)


def plus(keep, got):
    return keep.astype(F32) + got.astype(F32)


def row_half(total):
    rows = total.shape[0] // 2
    return total[:rows], swap(total[rows:].astype(BF16), "row")


def spread(total):
    count = lax.axis_size("dp")
    rows, cols = total.shape
    shares = total.astype(BF16).reshape(count, rows // count, cols)
    return lax.all_to_all(shares, "dp", 0, 0, tiled=True)


def collect(shares):
    count, rows, cols = shares.shape
    share = jnp.sum(shares.astype(F32), axis=0, keepdims=True).astype(BF16)
    whole = lax.all_to_all(jnp.broadcast_to(share, shares.shape), "dp", 0, 0, tiled=True)
    return whole.reshape(count * rows, cols)


def scale_of(values):
    return lax.rsqrt(jnp.mean(values * values, axis=-2, keepdims=True) + EPSILON)


def norm_backward(values, scale, offset, gradient):
    unit = values * scale
    scaled = gradient * (1.0 + offset)
    inner = jnp.mean(scaled * unit, axis=0, keepdims=True)
    return scale * (scaled - unit * inner), jnp.sum(gradient * unit, axis=1)


def rms_scale(values, offset):
    return values * scale_of(values) * (1.0 + offset)


def rotate(values, cosine, sine):
    half_dim = values.shape[-2] // 2
    first_half = values[..., :half_dim, :]
    second_half = values[..., half_dim:, :]
    return jnp.concatenate(
        [first_half * cosine - second_half * sine, second_half * cosine + first_half * sine],
        axis=-2,
    )


def rope_tables(first, count):
    half_dim = HEAD_DIM // 2
    frequency = ROPE_BASE ** (-(jnp.arange(half_dim, dtype=F32) * 2.0 / HEAD_DIM))
    angles = (first + jnp.arange(count, dtype=jnp.int32)).astype(F32)[None, :] * frequency[:, None]
    return (jnp.cos(angles), jnp.sin(angles))


def nn(a, b):
    return jnp.dot(a, b, preferred_element_type=F32)


def nt(a, b):
    return lax.dot_general(a, b, (((1,), (1,)), ((), ())), preferred_element_type=F32)


def tn(a, b):
    return lax.dot_general(a, b, (((0,), (0,)), ((), ())), preferred_element_type=F32)


def seen_mask(first_key):
    key = lax.broadcasted_iota(jnp.int32, (SPAN, BLOCK), 0)
    query = lax.broadcasted_iota(jnp.int32, (SPAN, BLOCK), 1)
    return (key > query) & (key <= query + WINDOW) & (key >= first_key)


def attend_kernel(first_ref, query_ref, key_ref, value_ref, out_ref):
    start = pl.multiple_of(pl.program_id(0) * BLOCK, BLOCK)
    keys = key_ref[:, pl.ds(start, SPAN)].T
    values = value_ref[:, pl.ds(start, SPAN)]
    mask = seen_mask(first_ref[0] - start)
    for head in range(HEADS):
        features = slice(head * HEAD_DIM, (head + 1) * HEAD_DIM)
        weights = jnp.where(mask, jnp.exp(nn(keys, query_ref[features, :])), 0.0)
        total = jnp.sum(weights, axis=0, keepdims=True)
        probs = (weights * (1.0 / total)).astype(BF16)
        out_ref[features, :] = nn(values, probs).astype(BF16)


def attend_back_kernel(first_ref, query_ref, key_ref, value_ref, grad_ref, query_out, key_out, value_out):
    block = pl.program_id(0)
    start = pl.multiple_of(block * BLOCK, BLOCK)
    window = pl.ds(start, SPAN)
    keys_wide = key_ref[:, window]
    keys = keys_wide.T
    values = value_ref[:, window].T
    mask = seen_mask(first_ref[0] - start)

    @pl.when(block == 0)
    def _():
        key_out[...] = jnp.zeros_like(key_out)
        value_out[...] = jnp.zeros_like(value_out)

    key_sum = key_out[:, window]
    value_sum = value_out[:, window]
    for head in range(HEADS):
        features = slice(head * HEAD_DIM, (head + 1) * HEAD_DIM)
        queries = query_ref[features, :]
        grads = grad_ref[features, :]
        weights = jnp.where(mask, jnp.exp(nn(keys, queries)), 0.0)
        probs = weights * (1.0 / jnp.sum(weights, axis=0, keepdims=True))
        prob_grad = nn(values, grads)
        inner = jnp.sum(prob_grad * probs, axis=0, keepdims=True)
        score_grad = (probs * (prob_grad - inner)).astype(BF16)
        query_out[features, :] = nn(keys_wide, score_grad)
        key_sum += nt(queries, score_grad)
        value_sum += nt(grads, probs.astype(BF16))
    key_out[:, window] = key_sum
    value_out[:, window] = value_sum


def attend_call(kernel, name, out_specs, out_shape, products, arrays):
    width, tokens = arrays[1].shape
    span = arrays[2].shape[1]
    block = pl.BlockSpec((width, BLOCK), lambda i: (0, i))
    whole = pl.BlockSpec((HEAD_DIM, span), lambda i: (0, 0))
    return pl.pallas_call(
        kernel,
        grid=(tokens // BLOCK,),
        in_specs=[pl.BlockSpec(memory_space=pltpu.SMEM), block, whole, whole] + [block] * (len(arrays) - 4),
        out_specs=[{"block": block, "whole": whole}[spec] for spec in out_specs],
        out_shape=out_shape,
        compiler_params=pltpu.CompilerParams(vmem_limit_bytes=20 << 20),
        cost_estimate=QUICK,
        name=name,
    )(*arrays)


def attend(first, queries, keys, values):
    shape = [jax.ShapeDtypeStruct(queries.shape, BF16)]
    return attend_call(attend_kernel, "attend", ["block"], shape, 2, (first, queries, keys, values))[0]


def attend_back(first, queries, keys, values, heads_grad):
    shapes = [jax.ShapeDtypeStruct(a.shape, F32) for a in (queries, keys, values)]
    return attend_call(
        attend_back_kernel,
        "attend_back",
        ["block", "whole", "whole"],
        shapes,
        5,
        (first, queries, keys, values, heads_grad),
    )


HIDDEN = 256
LANES = 128
GELU_SCALE = 0.7978845608028654
GELU_CUBE = 0.044715


def ffn_kernel(x_ref, gate_own, gate_far, up_own, up_far, down_own, down_far, gate_out, up_out, product_out, branch_out):
    x = x_ref[...]
    gate = tn(jnp.concatenate([gate_own[...], gate_far[...]], axis=0), x)
    up = tn(jnp.concatenate([up_own[...], up_far[...]], axis=0), x)
    bend = jnp.tanh(GELU_SCALE * (gate + GELU_CUBE * gate * gate * gate))
    product = (0.5 * gate * (1.0 + bend) * up).astype(BF16)
    gate_out[...] = gate.astype(BF16)
    up_out[...] = up.astype(BF16)
    product_out[...] = product
    part = nn(jnp.concatenate([down_own[...], down_far[...]], axis=0), product)

    @pl.when(pl.program_id(0) == 0)
    def _():
        branch_out[...] = part

    @pl.when(pl.program_id(0) > 0)
    def _():
        branch_out[...] += part


def ffn_back_kernel(
    x_ref,
    grad_ref,
    gate_ref,
    up_ref,
    product_ref,
    gate_own,
    gate_far,
    up_own,
    up_far,
    down_own,
    down_far,
    mid_out,
    weight_out,
):
    x = x_ref[...]
    grad = grad_ref[...]
    gate = gate_ref[...].astype(F32)
    up = up_ref[...].astype(F32)
    product_grad = tn(jnp.concatenate([down_own[...], down_far[...]], axis=0), grad)
    square = gate * gate
    bend = jnp.tanh(GELU_SCALE * gate * (1.0 + GELU_CUBE * square))
    rise = 0.5 * (1.0 + bend)
    slope = rise + (0.5 * GELU_SCALE) * gate * (1.0 - bend * bend) * (1.0 + (3.0 * GELU_CUBE) * square)
    gate_grad = (product_grad * up * slope).astype(BF16)
    up_grad = (product_grad * gate * rise).astype(BF16)
    kind = weight_out.dtype
    weight_out[0] = nt(grad, product_ref[...]).astype(kind)
    weight_out[1] = nt(x, gate_grad).astype(kind)
    weight_out[2] = nt(x, up_grad).astype(kind)
    part = nn(jnp.concatenate([gate_own[...], gate_far[...]], axis=0), gate_grad)
    part += nn(jnp.concatenate([up_own[...], up_far[...]], axis=0), up_grad)

    @pl.when(pl.program_id(0) == 0)
    def _():
        mid_out[...] = part

    @pl.when(pl.program_id(0) > 0)
    def _():
        mid_out[...] += part


def attend_weights_kernel(col_ref, x_ref, query_ref, keyval_ref, gain_ref, own_out, sent_out):
    x = x_ref[...]
    half = query_ref.shape[0] // 2
    col = col_ref[0]
    wide = jnp.concatenate([gain_ref[...], jnp.zeros((LANES - gain_ref.shape[0], D), F32)], axis=0)
    gains = wide.T
    for out, start, which in ((sent_out, half, 1 - col), (own_out, 0, col)):
        rows = pl.ds(pl.multiple_of(which * HEAD_DIM, HEAD_DIM), HEAD_DIM)
        out[:, :half] = nt(x, query_ref[start : start + half, :]).astype(out.dtype)
        out[:, half : half + HEAD_DIM] = nt(x, keyval_ref[rows, :]).astype(out.dtype)
        out[:, half + HEAD_DIM :] = gains.astype(out.dtype)


def attend_weights(col, x, query_grad, keyval_grad, gain_grads):
    width = query_grad.shape[0] // 2 + HEAD_DIM + LANES
    vmem = pl.BlockSpec(memory_space=pltpu.VMEM)
    return pl.pallas_call(
        attend_weights_kernel,
        in_specs=[pl.BlockSpec(memory_space=pltpu.SMEM), vmem, vmem, vmem, vmem],
        out_specs=[vmem, vmem],
        out_shape=[jax.ShapeDtypeStruct((D, width), F32), jax.ShapeDtypeStruct((D, width), BF16)],
        compiler_params=pltpu.CompilerParams(vmem_limit_bytes=24 << 20),
        cost_estimate=QUICK,
        name="attend_weights",
    )(col.astype(jnp.int32).reshape(1), x, query_grad, keyval_grad, gain_grads)


def far(values):
    return pltpu.with_memory_space_constraint(values, pltpu.HBM)


def weight_specs(weights):
    specs = []
    for array, first in weights:
        specs.append(pl.BlockSpec((array.shape[0], HIDDEN), lambda i, first=first: (0, first // HIDDEN + i)))
    return specs


def ffn(x, weights, hidden):
    tokens = x.shape[1]
    rows = pl.BlockSpec((HIDDEN, tokens), lambda i: (i, 0))
    whole = pl.BlockSpec(x.shape, lambda i: (0, 0))
    once = pl.BlockSpec(x.shape, lambda i: (0, 0), pipeline_mode=pl.Buffered(1))
    wide = pltpu.HBM((hidden, tokens), BF16)
    return pl.pallas_call(
        ffn_kernel,
        grid=(hidden // HIDDEN,),
        in_specs=[once] + weight_specs(weights),
        out_specs=[rows, rows, rows, whole],
        out_shape=[wide, wide, wide, jax.ShapeDtypeStruct(x.shape, F32)],
        compiler_params=pltpu.CompilerParams(vmem_limit_bytes=24 << 20),
        cost_estimate=SLOW,
        name="ffn",
    )(x, *(far(array) for array, _ in weights))


def ffn_back(x, grad, gate, up, product, weights, hidden, kind):
    tokens = x.shape[1]
    rows = pl.BlockSpec((HIDDEN, tokens), lambda i: (i, 0))
    whole = pl.BlockSpec(x.shape, lambda i: (0, 0))
    once = pl.BlockSpec(x.shape, lambda i: (0, 0), pipeline_mode=pl.Buffered(1))
    column = pl.BlockSpec((3, D, HIDDEN), lambda i: (0, 0, i))
    weight = pltpu.HBM((3, D, hidden), kind)
    return pl.pallas_call(
        ffn_back_kernel,
        grid=(hidden // HIDDEN,),
        in_specs=[once, once, rows, rows, rows] + weight_specs(weights),
        out_specs=[whole, column],
        out_shape=[jax.ShapeDtypeStruct(x.shape, F32), weight],
        compiler_params=pltpu.CompilerParams(vmem_limit_bytes=28 << 20),
        cost_estimate=SLOW,
        name="ffn_back",
    )(*(far(array) for array in (x, grad, gate, up, product)), *(far(array) for array, _ in weights))


def per_device(
    inputs,
    cotangent,
    query_weight,
    keyval_weight,
    out_weight,
    gate_weight,
    up_weight,
    down_weight,
    attend_in_gain,
    attend_out_gain,
    forward_in_gain,
    forward_out_gain,
    query_gain,
    key_gain,
):
    assert inputs.shape[0] == LEN
    row = lax.axis_index("row")
    col = lax.axis_index("col")
    part = row * 2 + col
    tokens = LEN // PARTS
    ahead = [(i, i + 1) for i in range(PARTS - 1)]
    behind = [(i + 1, i) for i in range(PARTS - 1)]
    half = HEADS * HEAD_DIM // 2

    unit = gate_weight.shape[1]

    low = to_tokens(inputs.T, part, col)
    pack = jnp.concatenate([query_weight, keyval_weight], axis=1)
    pack_other = swap(pack, "row")
    query_col = swap(query_weight, "col")
    gains = jnp.stack([attend_in_gain, attend_out_gain, forward_in_gain, forward_out_gain])
    gains = gather_gains(gains, col)
    in_gain, out_gain, mid_gain, last_gain = (gains[i][:, None] for i in range(4))
    query_gain, key_gain = query_gain[:, None], key_gain[:, None]
    cosine, sine = rope_tables(part * tokens, tokens)
    first = jnp.where(part == 0, WINDOW, 0).astype(jnp.int32).reshape(1)

    rest = jnp.concatenate([out_weight.T, gate_weight, up_weight, down_weight.T], axis=1)
    rest_col = swap(rest, "col")
    at_gate, at_up, at_down = half, half + unit, half + 2 * unit
    rest_half = half_of(rest[:, :at_down], bit_of(1), 0)
    low, out_half = pin(low, rest_half[:, :at_up])
    out_row = swap(out_half, "row")
    pack_other, up_half = pin(pack_other, rest_half[:, at_up:at_down])
    up_row = swap(up_half, "row")
    query_other = pack_other[:, :half]
    query_full = grid4(query_weight, query_col, query_other, swap(query_other, "col"))
    keyval_full = jnp.concatenate([keyval_weight, pack_other[:, half:]], axis=0)

    residual = low.astype(F32)
    scale_in = scale_of(residual)
    attend_in = (residual * scale_in * (1.0 + in_gain)).astype(BF16)
    keyval_raw = tn(keyval_full, attend_in)
    key_raw = keyval_raw[:HEAD_DIM]
    value_rows = keyval_raw[HEAD_DIM:].astype(BF16)

    def query_prep(raw, gain):
        return rotate(rms_scale(raw, gain), cosine, sine) * HEAD_DIM ** (-0.5)

    def key_prep(raw, gain):
        return rotate(rms_scale(raw, gain), cosine, sine)

    key_ready, key_pullback = jax.vjp(key_prep, key_raw, key_gain)
    key_rows = key_ready.astype(BF16)
    halo = lax.ppermute(
        jnp.concatenate([key_rows[:, tokens - WINDOW :], value_rows[:, tokens - WINDOW :]], axis=0),
        ("row", "col"),
        ahead,
    )
    query_raw = tn(query_full, attend_in).reshape(HEADS, HEAD_DIM, tokens)
    query_ready, query_pullback = jax.vjp(query_prep, query_raw, query_gain)
    query_rows = query_ready.astype(BF16).reshape(HEADS * HEAD_DIM, tokens)
    query_rows, halo, out_row, down_half = pin(query_rows, halo, out_row, half_of(rest[:, at_down:], bit_of(2), 0))
    out_there = swap_dp(out_row, 1)
    down_row = swap(down_half, "row")
    keys = jnp.concatenate([halo[:HEAD_DIM], key_rows], axis=1)
    values = jnp.concatenate([halo[HEAD_DIM:], value_rows], axis=1)
    mixed_heads = attend(first, query_rows, keys, values)
    mixed_heads, out_there, up_row, down_row, cot = pin(mixed_heads, out_there, up_row, down_row, cotangent.T)
    out_far = ordered(bit_of(1), out_row, out_there, 0)
    out_far_col = swap(out_far, "col")
    up_there = swap_dp(up_row, 1)

    out_full = grid4(rest[:, :half], rest_col[:, :half], out_far[:, :half], out_far_col[:, :half])
    branch_attn = nn(out_full, mixed_heads)
    down_there = swap_dp(down_row, 2)
    branch_attn, up_there, cot = pin(branch_attn, up_there, cot)
    upstream = to_tokens(cot, part, col)
    up_far = ordered(bit_of(1), up_row, up_there, 0)
    up_far_col = swap(up_far, "col")
    scale_attn = scale_of(branch_attn)
    hidden_state = residual + branch_attn * scale_attn * (1.0 + out_gain)
    scale_mid = scale_of(hidden_state)
    forward_in = (hidden_state * scale_mid * (1.0 + mid_gain)).astype(BF16)
    forward_in, down_there = pin(forward_in, down_there)
    down_far = ordered(bit_of(2), down_row, down_there, 0)
    down_far_col = swap(down_far, "col")
    own = ((rest, at_gate), (out_far, at_gate), (rest, at_up), (up_far, 0), (rest, at_down), (down_far, 0))
    other = (
        (rest_col, at_gate),
        (out_far_col, at_gate),
        (rest_col, at_up),
        (up_far_col, 0),
        (rest_col, at_down),
        (down_far_col, 0),
    )
    gate_own, up_own, product_own, branch_own = ffn(forward_in, own, unit)
    forward_in, branch_own, down_far_col = pin(forward_in, branch_own, down_far_col)
    other = other[:5] + ((down_far_col, 0),)
    gate_other, up_other, product_other, branch_other = ffn(forward_in, other, unit)
    branch_ffn = branch_own + branch_other
    scale_out = scale_of(branch_ffn)
    output = (hidden_state + branch_ffn * scale_out * (1.0 + last_gain)).astype(BF16)

    branch_ffn, upstream = pin(branch_ffn, upstream)
    upstream = upstream.astype(F32)
    output_got = send_features(output, col)
    ffn_grad, last_gain_grad = norm_backward(branch_ffn, scale_out, last_gain, upstream)
    ffn_grad = ffn_grad.astype(BF16)
    mid_other, sent1 = ffn_back(forward_in, ffn_grad, gate_other, up_other, product_other, other, unit, BF16)
    got1 = swap(sent1, "col")
    mid_other, ffn_grad, *output_got = pin(mid_other, ffn_grad, *output_got)
    mid_own, own1 = ffn_back(forward_in, ffn_grad, gate_own, up_own, product_own, own, unit, BF16)
    mid_own, got1 = pin(mid_own, got1)
    low_gate, high_gate = own1[1][:, : unit // 2], own1[1][:, unit // 2 :]
    low_got, high_got = got1[1][:, : unit // 2], got1[1][:, unit // 2 :]
    keep1, got1_a = row_half(jnp.concatenate([plus(own1[0], got1[0]), plus(low_gate, low_got)], axis=1))
    keep2, got2_a = dp_half(jnp.concatenate([plus(high_gate, high_got), plus(own1[2], got1[2])], axis=1), 2)

    mid_grad = mid_own + mid_other
    state_part, mid_gain_grad = norm_backward(hidden_state, scale_mid, mid_gain, mid_grad)
    state_grad = upstream + state_part
    attn_grad, out_gain_grad = norm_backward(branch_attn, scale_attn, out_gain, state_grad)
    attn_grad = attn_grad.astype(BF16)
    got_out = swap(nt(attn_grad, mixed_heads[half:]).astype(BF16), "col")
    own_out = nt(attn_grad, mixed_heads[:half])
    heads_grad = tn(out_full, attn_grad).astype(BF16)

    query_back, key_back, value_back = attend_back(first, query_rows, keys, values, heads_grad)
    back = lax.ppermute(
        jnp.concatenate([key_back[:, :WINDOW], value_back[:, :WINDOW]], axis=0).astype(BF16),
        ("row", "col"),
        behind,
    )
    query_back, got_out, own_out, got1_a, got2_a = pin(query_back, got_out, own_out, got1_a, got2_a)
    keep1, got1_b = dp_half(plus(keep1, got1_a), 1)
    keep2, got2_b = row_half(plus(keep2, got2_a))
    keep_out, got_out = row_half(plus(own_out, got_out))
    query_raw_grad, query_gain_grad = query_pullback(query_back.reshape(HEADS, HEAD_DIM, tokens))
    query_raw_grad = query_raw_grad.reshape(HEADS * HEAD_DIM, tokens).astype(BF16)
    in_query = nn(query_full, query_raw_grad)
    in_query, back, got1_b = pin(in_query, back, got1_b)
    keep1, got1_c = dp_half(plus(keep1, got1_b), 2)

    spare = tokens - WINDOW
    back = jnp.pad(back.astype(F32), ((0, 0), (spare, 0)))
    key_raw_grad, key_gain_grad = key_pullback(key_back[:, WINDOW:] + back[:HEAD_DIM])
    value_grad = value_back[:, WINDOW:] + back[HEAD_DIM:]
    keyval_raw_grad = jnp.concatenate([key_raw_grad, value_grad], axis=0).astype(BF16)
    in_grad = in_query + nn(keyval_full, keyval_raw_grad)
    in_grad, got2_b, got_out = pin(in_grad, got2_b, got_out)
    keep2, keep_out = plus(keep2, got2_b), plus(keep_out, got_out)
    width2, width_out = keep2.shape[1] // 2, half // 2
    keep2, got2_c = dp_half(
        jnp.concatenate(
            [keep2[:, :width2], keep_out[:, :width_out], keep2[:, width2:], keep_out[:, width_out:]], axis=1
        ),
        1,
    )
    residual_part, in_gain_grad = norm_backward(residual, scale_in, in_gain, in_grad)

    pad = jnp.zeros((D // 2 - HEAD_DIM,), F32)
    query_gain_grad, key_gain_grad = query_gain_grad[:, 0], key_gain_grad[:, 0]
    gain_grads = jnp.stack(
        [
            in_gain_grad,
            out_gain_grad,
            mid_gain_grad,
            last_gain_grad,
            jnp.concatenate([query_gain_grad, pad, query_gain_grad, pad]),
            jnp.concatenate([key_gain_grad, pad, key_gain_grad, pad]),
            jnp.zeros((D,), F32),
            jnp.zeros((D,), F32),
        ]
    )
    input_grad = (state_grad + residual_part).astype(BF16)
    own3, sent3 = attend_weights(col, attend_in, query_raw_grad, keyval_raw_grad, gain_grads)
    got3 = swap(sent3, "col")
    own3, got3 = pin(own3, got3)
    keep3, got3 = row_half(plus(own3, got3))
    keep1, keep2 = plus(keep1, got1_c), plus(keep2, got2_c)
    width1 = keep1.shape[1]
    keep12 = jnp.concatenate([keep1, keep2[:, :width2]], axis=1)
    share_out = keep2[:, width2:].astype(BF16)
    there_out = swap_dp(share_out, 2)
    bits = dp_bits()[2:]
    for bit in bits[:-1]:
        keep12 = plus(*dp_half(keep12, bit, 0))
    if bits:
        keep12, got12 = dp_half(keep12, bits[-1], 0)

    got3, got12, there_out, input_grad = pin(got3, got12, there_out, input_grad)
    shares3 = spread(plus(keep3, got3))
    input_got = send_features(input_grad, col)
    half12 = plus(keep12, got12).astype(BF16)
    for bit in reversed(bits):
        half12 = dp_back(half12, bit, 0)
    for bit in bits:
        share_out = plus(share_out.astype(F32), there_out).astype(BF16)
        there_out = swap_dp(share_out, bit)
    share_out = plus(share_out.astype(F32), there_out).astype(BF16)
    half12, share_out = pin(half12, share_out)
    half1, half2 = half12[:, :width1], jnp.concatenate([half12[:, width1:], share_out], axis=1)
    there1, there2 = swap_dp(half1, 2), swap_dp(half2, 1)
    whole1 = ordered(bit_of(2), half1, there1, 1)
    whole2 = ordered(bit_of(1), half2[:, :width2], there2[:, :width2], 1)
    whole_out = ordered(bit_of(1), half2[:, width2:], there2[:, width2:], 1)
    there1, there2 = swap_dp(whole1, 1), swap_dp(whole2, 2)
    shares3, *input_got = pin(shares3, *input_got)
    whole3 = collect(shares3)
    whole1 = ordered(bit_of(1), whole1, there1, 1)
    whole2 = ordered(bit_of(2), whole2, there2, 1)
    down_grad, gate_low = whole1[:, :unit], whole1[:, unit:]
    gate_high, up_grad = whole2[:, : unit // 2], whole2[:, unit // 2 :]
    gate_grad = jnp.concatenate([gate_low, gate_high], axis=1)

    keyval_mine = whole3[:, half : half + HEAD_DIM]
    keyval_grad = ordered(col, keyval_mine, swap(keyval_mine, "col"), 1)
    gain_all = whole3[:, half + HEAD_DIM :].astype(F32)
    gain_mine = half_of(gain_all, col, 0)
    output = join_features(output_got, part)
    input_grad = join_features(input_got, part)
    return (
        output.T,
        input_grad.T.astype(F32),
        whole3[:, :half].astype(F32),
        keyval_grad.astype(F32),
        whole_out.T.astype(F32),
        gate_grad.astype(F32),
        up_grad.astype(F32),
        down_grad.T.astype(F32),
        gain_mine[:, 0],
        gain_mine[:, 1],
        gain_mine[:, 2],
        gain_mine[:, 3],
        gain_all[:HEAD_DIM, 4],
        gain_all[:HEAD_DIM, 5],
    )


def solution(mesh):
    wide = P("dp", ("row", "col"))
    gain = P(("row", "col"))
    weights = (P("row", "col"), P("row", None), P("col", "row"), P("row", "col"), P("row", "col"), P("col", "row"))
    gains = (gain, gain, gain, gain, P(), P())
    return jax.shard_map(
        per_device,
        mesh=mesh,
        in_specs=(wide, wide) + weights + gains,
        out_specs=(wide, wide) + weights + gains,
        check_vma=False,
    )
```
